256 devices in a mesh: gx: 32 (over z, x), gy: 8 (over y, core).
Axes of the slice: x: 4, y: 4, z: 8, core: 2. Of those that a mesh axis runs over, the one named last changes fastest.
Arguments:
- state_field: float32 [4, 1024, 4096], P(None, 'gx', 'gy'), may hold values from -4 to 4
- x_coupling: bfloat16 [4, 1024, 4096], P(None, 'gx', 'gy'), may hold values from 9984 to 99840
- y_coupling: bfloat16 [4, 1024, 4096], P(None, 'gx', 'gy'), may hold values from 0.049804688 to 0.5
- cross_coeff: bfloat16 [4, 1024, 4096], P(None, 'gx', 'gy'), may hold values from -0.29882812 to 0.29882812
Outputs:
- solved_field: float32 [4, 1024, 4096], P(None, 'gx', 'gy')
- right_side: float32 [4, 1024, 4096], P(None, 'gx', 'gy')
The draws below stay inside these ranges and needn't reach their ends.
All inputs are finite; a program needn't handle non-finite values.
Results may differ from the reference program's by a relative error of at most 0.0009.
Values sent between devices are 32-bit elements; how exact they have to be, the bound alone decides.
A program may use at most 64 MiB of HBM per device.

```python
import math
import jax
import jax.numpy as jnp
from jax import lax

PLANES = 4
NX = 1024
NY = 4096


def draw_state_field(key, part):
    key = jax.random.fold_in(key, 11)
    shape = (PLANES, NX, NY)
    return jnp.clip(jax.random.normal(key, shape, jnp.float32) + 0.5, -4.0, 4.0)


def levels(own_key, dims, shards, low, top_value):
    gain, own = 1.0, jax.random.fold_in(own_key, 6)
    for dim, parts in shards:
        heights = jnp.exp(jax.random.uniform(jax.random.fold_in(own, dim), (parts,), jnp.float32, low / len(shards), top_value / len(shards)))
        gain = gain * jnp.repeat(heights, dims[dim] // parts).reshape([-1 if axis == dim else 1 for axis in range(len(dims))])
    return gain


def setup_inputs(seed: int = 0) -> dict:
    splits = jax.random.split(jax.random.key(seed), 5)
    state_field = draw_state_field(jax.random.fold_in(splits[4], 71), 0)
    x_coupling = jnp.clip(jnp.exp(math.log(99840.0) - 2.3025851 * jax.random.uniform(splits[1], (PLANES, NX, NY), jnp.float32) ** levels(splits[1], (PLANES, NX, NY), ((1, 32), (2, 8)), -0.2, 0.2)), 9984.0, 99840.0).astype(jnp.bfloat16)
    y_coupling = jnp.clip(jnp.exp(math.log(0.5) - 2.306499 * jax.random.uniform(splits[2], (PLANES, NX, NY), jnp.float32) ** levels(splits[2], (PLANES, NX, NY), ((1, 32), (2, 8)), -0.2, 0.2)), 0.049804688, 0.5).astype(jnp.bfloat16)
    cross_coeff = jnp.clip(jax.random.uniform(splits[3], (PLANES, NX, NY), jnp.float32, -0.29882812, 0.29882812) * levels(splits[3], (PLANES, NX, NY), ((1, 32), (2, 8)), -0.4, 0.0), -0.29882812, 0.29882812).astype(jnp.bfloat16)
    return dict(state_field=state_field, x_coupling=x_coupling, y_coupling=y_coupling, cross_coeff=cross_coeff)


def thomas_solve(lower_band, center_band, upper_band, source):
    width_zero = jnp.zeros(source.shape[1:], jnp.float32)

    def forward(carried, row_data):
        prev_upper, prev_source = carried
        low_row, cen_row, upp_row, src_row = row_data
        pivot_value = cen_row - low_row * prev_upper
        new_upper = upp_row / pivot_value
        new_source = (src_row - low_row * prev_source) / pivot_value
        return (new_upper, new_source), (new_upper, new_source)

    carried, outputs = lax.scan(forward, (width_zero, width_zero), (lower_band, center_band, upper_band, source))
    ratios, partial_values = outputs

    def backward(next_value, row_data):
        ratio_row, part_row = row_data
        value_row = part_row - ratio_row * next_value
        return value_row, value_row

    carried_back, solved_values = lax.scan(backward, width_zero, (ratios, partial_values), reverse=True)
    return solved_values


def one_plane(plane_data):
    state_plane, x_plane, y_plane, cross_plane = plane_data
    x_local = x_plane.astype(jnp.float32)
    y_local = y_plane.astype(jnp.float32)
    cross_local = cross_plane.astype(jnp.float32)
    padded = jnp.pad(state_plane, 1)
    y_before = jnp.pad(y_local, ((0, 0), (1, 0)))[:, :-1]
    second_y = y_local * (padded[1:-1, 2:] - state_plane) - y_before * (state_plane - padded[1:-1, :-2])
    mixed_term = cross_local * (padded[2:, 2:] - padded[2:, :-2] - padded[:-2, 2:] + padded[:-2, :-2]) * 0.25
    right_plane = state_plane + second_y + mixed_term
    x_before = jnp.pad(x_local, ((1, 0), (0, 0)))[:-1]
    solved_plane = thomas_solve(-x_before, 1.0 + x_before + x_local, -x_local, right_plane)
    return solved_plane, right_plane


def reference(state_field, x_coupling, y_coupling, cross_coeff):
    solved_field, right_side = lax.map(one_plane, (state_field, x_coupling, y_coupling, cross_coeff))
    return solved_field, right_side
```

```python
import jax
import jax.numpy as jnp
from jax import lax
from jax.experimental import pallas as pl
from jax.experimental.pallas import tpu as pltpu
from jax.sharding import PartitionSpec as P

MESH = pl.DeviceIdType.MESH
PL = 4
R = 32
W = 512
NB = 32
NS = 4
NV = 6


def sweep_kernel(u_ref, kx_ref, ky_ref, g_ref, o_ref, r_ref,
                 rows_s, cols_s, hrow, hcol, hcor,
                 ik_s, r_s, a_s, b_s, v_s, msg, inbox, res, xf,
                 hs, hr, ms, mr, rs, rr):
    me = lax.axis_index("gx")
    gy = lax.axis_index("gy")
    prev, nxt = lax.rem(me + NB - 1, NB), lax.rem(me + 1, NB)
    west, east = lax.rem(gy + 7, 8), lax.rem(gy + 1, 8)

    def signal(dev):
        pl.semaphore_signal(barrier, inc=1, device_id=dev, device_id_type=MESH)

    barrier = pltpu.get_barrier_semaphore()
    is_solver = me < NS

    @pl.when(is_solver)
    def _():
        for k in range(1, NB):
            signal((lax.rem(me + k, NB), gy))

    for dev in ((prev, gy), (nxt, gy), (me, west), (me, east),
                (prev, west), (prev, east), (nxt, west), (nxt, east)):
        signal(dev)

    lane = lax.broadcasted_iota(jnp.int32, (8, 128), 1)
    for p in range(PL):
        rows_s[0, p:p + 1, :] = u_ref[R * p:R * p + 1, :]
        rows_s[1, p:p + 1, :] = u_ref[R * p + R - 1:R * p + R, :]
    kyf = ky_ref[...].astype(jnp.float32)
    to_east = jnp.zeros((8, 128), jnp.float32)
    to_west = jnp.zeros((8, 128), jnp.float32)
    for m in range(16):
        sl = slice(8 * m, 8 * m + 8)
        to_east = jnp.where(lane == m, pltpu.roll(u_ref[sl, 384:512], (m + 1) % 128, 1), to_east)
        to_east = jnp.where(lane == 16 + m, pltpu.roll(kyf[sl, 384:512], (m + 17) % 128, 1), to_east)
        to_west = jnp.where(lane == m, pltpu.roll(u_ref[sl, 0:128], m, 1) if m else u_ref[sl, 0:128], to_west)
    cols_s[0] = to_east
    cols_s[1] = to_west

    pl.semaphore_wait(barrier, 8 + NS - is_solver.astype(jnp.int32))

    def send(src, dst, i, dev):
        c = pltpu.make_async_remote_copy(src_ref=src, dst_ref=dst, send_sem=hs.at[i], recv_sem=hr.at[i],
                                         device_id=dev, device_id_type=MESH)
        c.start()
        return c

    halos = [
        send(rows_s.at[1], hrow.at[0], 0, (nxt, gy)),
        send(rows_s.at[0], hrow.at[1], 1, (prev, gy)),
        send(cols_s.at[0], hcol.at[0], 2, (me, east)),
        send(cols_s.at[1], hcol.at[1], 3, (me, west)),
        send(rows_s.at[1, :, pl.ds(384, 128)], hcor.at[0], 4, (nxt, east)),
        send(rows_s.at[1, :, pl.ds(0, 128)], hcor.at[1], 5, (nxt, west)),
        send(rows_s.at[0, :, pl.ds(384, 128)], hcor.at[2], 6, (prev, east)),
        send(rows_s.at[0, :, pl.ds(0, 128)], hcor.at[3], 7, (prev, west)),
    ]

    ik = 1.0 / kx_ref[...].astype(jnp.float32)
    for q in range(NS):
        ik_s[128 * q:128 * q + 128, :] = ik[:, 128 * q:128 * q + 128]
    a = d = jnp.ones((16, 128), jnp.float32)
    b = c = jnp.zeros((16, 128), jnp.float32)
    for i in range(R):
        row = pl.ds(i, 16, stride=R)
        a_s[row, :] = a
        b_s[row, :] = b
        ik = ik_s[row, :]
        c = c + a
        a = a + c * ik
        d = d + b
        b = b + d * ik

    def put(k, value):
        for q in range(NS):
            msg[q, 4 * k:4 * k + 4, :] = value[4 * q:4 * q + 4, :]

    for k, value in enumerate((a, b, c, d)):
        put(k, value)

    for h in halos:
        h.wait()

    lane_w = lax.broadcasted_iota(jnp.int32, (R, W), 1)
    row_w = lax.broadcasted_iota(jnp.int32, (R, W), 0)
    lane_p = lax.broadcasted_iota(jnp.int32, (PL, W), 1)
    col_w = jnp.where(gy == 0, 0.0, hcol[0])
    col_e = jnp.where(gy == 7, 0.0, hcol[1])

    def wide(tile, at_end):
        rest = jnp.zeros((tile.shape[0], W - 128), jnp.float32)
        return jnp.concatenate([rest, tile] if at_end else [tile, rest], axis=1)

    def halo_diff(row, cor_w, cor_e, missing):
        cw = jnp.where(gy == 0, 0.0, cor_w)
        ce = jnp.where(gy == 7, 0.0, cor_e)
        w = jnp.where(lane_p == 0, wide(pltpu.roll(cw, 1, 1), False), pltpu.roll(row, 1, 1))
        e = jnp.where(lane_p == W - 1, wide(pltpu.roll(ce, 127, 1), True), pltpu.roll(row, W - 1, 1))
        return jnp.where(missing, 0.0, e - w)

    d_prev = halo_diff(hrow[0], hcor[0], hcor[1], me == 0)
    d_next = halo_diff(hrow[1], hcor[2], hcor[3], me == NB - 1)

    for p in range(PL):
        sl = slice(R * p, R * p + R)
        u = u_ref[sl, :]
        ky = ky_ref[sl, :].astype(jnp.float32)
        g = g_ref[sl, :].astype(jnp.float32)
        cw, ck, ce = [], [], []
        for q in range(4):
            m = 4 * p + q
            cw.append(pltpu.roll(col_w, 128 - m, 1) if m else col_w)
            ck.append(pltpu.roll(col_w, 112 - m, 1))
            ce.append(pltpu.roll(col_e, 127 - m, 1))
        cw, ck, ce = (jnp.concatenate(t, axis=0) for t in (cw, ck, ce))
        uw = jnp.where(lane_w == 0, wide(cw, False), pltpu.roll(u, 1, 1))
        kb = jnp.where(lane_w == 0, wide(ck, False), pltpu.roll(ky, 1, 1))
        ue = jnp.where(lane_w == W - 1, wide(ce, True), pltpu.roll(u, W - 1, 1))
        dd = ue - uw
        up = jnp.where(row_w == 0, d_prev[p:p + 1, :], pltpu.roll(dd, 1, 0))
        dn = jnp.where(row_w == R - 1, d_next[p:p + 1, :], pltpu.roll(dd, R - 1, 0))
        right = u + (ky * (ue - u) - kb * (u - uw)) + g * (dn - up) * 0.25
        r_ref[sl, :] = right
        for q in range(NS):
            r_s[128 * q + R * p:128 * q + R * p + R, :] = right[:, 128 * q:128 * q + 128]

    vx = vf = jnp.zeros((16, 128), jnp.float32)
    for i in range(R):
        row = pl.ds(i, 16, stride=R)
        v_s[row, :] = vx
        vf = vf + (vx - r_s[row, :])
        vx = vx + vf * ik_s[row, :]
    put(4, vx)
    put(5, vf)

    def map_copy(s):
        return pltpu.make_async_remote_copy(
            src_ref=msg.at[s],
            dst_ref=inbox.at[me],
            send_sem=ms.at[s], recv_sem=mr, device_id=(s, gy), device_id_type=MESH)

    for s in range(NS):
        @pl.when(me != s)
        def _():
            map_copy(s).start()

    @pl.when(is_solver)
    def _():
        for s in range(NS):
            @pl.when(me == s)
            def _():
                inbox[s] = msg[s]
        part = inbox.at[pl.ds(0, NB - 1)]
        pltpu.make_async_copy(part, part, mr).wait()

        def block(p):
            return [inbox[p, 4 * k:4 * k + 4, :] for k in range(NV)]

        groups = []
        for z in range(8):
            a, b, c, d, vx, vf = block(4 * z)
            for x in range(1, 4):
                a2, b2, c2, d2, vx2, vf2 = block(4 * z + x)
                a, c = a2 * a + b2 * c, c2 * a + d2 * c
                b, d = a2 * b + b2 * d, c2 * b + d2 * d
                vx, vf = a2 * vx + b2 * vf + vx2, c2 * vx + d2 * vf + vf2
            groups.append((a, b, c, d, vx, vf))
        zero = jnp.zeros((PL, 128), jnp.float32)
        left = [(zero, zero)]
        for z in range(7):
            a, b, c, d, vx, vf = groups[z]
            gl, jl = left[-1]
            inv = 1.0 / (a + b * gl)
            gn = (c + d * gl) * inv
            left.append((gn, jl * inv + vf - gn * vx))
        a, b, c, d, vx, vf = groups[7]
        inv = 1.0 / b
        right = [(a * inv, -vx * inv)]
        for z in range(6, -1, -1):
            a, b, c, d, vx, vf = groups[z]
            gr, jr = right[0]
            inv = 1.0 / (d + gr * b)
            right.insert(0, ((c + gr * a) * inv, (jr - vf - gr * vx) * inv))
        for z in range(8):
            gl, jl = left[z]
            gr, jr = right[z]
            x0 = (jr - jl) / (gl + gr)
            f0 = gl * x0 + jl
            for x in range(4):
                p = 4 * z + x
                res[p, 0:4, :] = x0
                res[p, 4:8, :] = f0
                if x < 3:
                    a, b, c, d, vx, vf = block(p)
                    x0, f0 = a * x0 + b * f0 + vx, c * x0 + d * f0 + vf

        for k in range(1, NB):
            p = lax.rem(me + k, NB)
            pltpu.make_async_remote_copy(
                src_ref=res.at[p], dst_ref=xf.at[me],
                send_sem=rs, recv_sem=rr.at[me], device_id=(p, gy), device_id_type=MESH).start()
        for s in range(NS):
            @pl.when(me == s)
            def _():
                xf[s] = res[s]

    for s in range(NS):
        @pl.when(me != s)
        def _():
            pltpu.make_async_copy(xf.at[s], xf.at[s], rr.at[s]).wait()

    for s in range(NS):
        ls = slice(128 * s, 128 * s + 128)
        for p in range(PL):
            sl = slice(R * p, R * p + R)
            x0 = xf[s, p:p + 1, :]
            f0 = xf[s, 4 + p:5 + p, :]
            ts = slice(128 * s + R * p, 128 * s + R * p + R)
            o_ref[sl, ls] = a_s[ts, :] * x0 + b_s[ts, :] * f0 + v_s[ts, :]

    for s in range(NS):
        @pl.when(me != s)
        def _():
            map_copy(s).wait_send()

    @pl.when(is_solver)
    def _():
        part = res.at[pl.ds(0, NB - 1)]
        pltpu.make_async_copy(part, part, rs).wait()


def shards(state_field, x_coupling, y_coupling, cross_coeff):
    flat = (PL * R, W)
    vmem = pl.BlockSpec(memory_space=pltpu.VMEM)
    f32 = jnp.float32
    big = pltpu.VMEM((NS * PL * R, 128), f32)
    dma = pltpu.SemaphoreType.DMA
    out, rhs = pl.pallas_call(
        sweep_kernel,
        out_shape=(jax.ShapeDtypeStruct(flat, f32),) * 2,
        in_specs=[vmem] * 4,
        out_specs=(vmem, vmem),
        scratch_shapes=[
            pltpu.VMEM((2, PL, W), f32), pltpu.VMEM((2, 8, 128), f32),
            pltpu.VMEM((2, PL, W), f32), pltpu.VMEM((2, 8, 128), f32), pltpu.VMEM((4, PL, 128), f32),
            big, big, big, big, big,
            pltpu.VMEM((NS, PL * NV, 128), f32), pltpu.VMEM((NB, PL * NV, 128), f32),
            pltpu.VMEM((NB, 8, 128), f32), pltpu.VMEM((NS, 8, 128), f32),
            dma((8,)), dma((8,)), dma((NS,)), dma(()), dma(()), dma((NS,)),
        ],
        compiler_params=pltpu.CompilerParams(
            collective_id=0, has_side_effects=True, vmem_limit_bytes=32 * 2**20),
    )(state_field.reshape(flat), x_coupling.reshape(flat), y_coupling.reshape(flat), cross_coeff.reshape(flat))
    return out.reshape(state_field.shape), rhs.reshape(state_field.shape)


def solution(mesh):
    spec = P(None, "gx", "gy")
    return jax.shard_map(shards, mesh=mesh, in_specs=(spec,) * 4, out_specs=(spec, spec), check_vma=False)
```

```python
import jax
import jax.numpy as jnp
from jax import lax
from jax.experimental import pallas as pl
from jax.experimental.pallas import tpu as pltpu
from jax.sharding import PartitionSpec as P

MESH = pl.DeviceIdType.MESH
PL = 4
R = 32
W = 512
NB = 32
NS = 4
NV = 6


def sweep_kernel(u_hbm, kx_hbm, ky_hbm, g_hbm, r_ref, a_s, b_s, v_s, xf,
                 u_ref, kx_ref, ky_ref, g_ref,
                 rows_s, cols_s, hrow, hcol, hcor,
                 ik_s, r_s, msg, inbox, res,
                 ls, hs, hr, ms, mr, rs, rr):
    loads = [pltpu.make_async_copy(src, dst, ls.at[i]) for i, (src, dst) in enumerate(
        ((u_hbm, u_ref), (ky_hbm, ky_ref), (kx_hbm, kx_ref), (g_hbm, g_ref)))]
    for load in loads:
        load.start()
    me = lax.axis_index("gx")
    gy = lax.axis_index("gy")
    prev, nxt = lax.rem(me + NB - 1, NB), lax.rem(me + 1, NB)
    west, east = lax.rem(gy + 7, 8), lax.rem(gy + 1, 8)

    def signal(dev):
        pl.semaphore_signal(barrier, inc=1, device_id=dev, device_id_type=MESH)

    barrier = pltpu.get_barrier_semaphore()
    is_solver = me < NS

    @pl.when(is_solver)
    def _():
        for k in range(1, NB):
            signal((lax.rem(me + k, NB), gy))

    for dev in ((prev, gy), (nxt, gy), (me, west), (me, east),
                (prev, west), (prev, east), (nxt, west), (nxt, east)):
        signal(dev)

    loads[0].wait()
    loads[1].wait()

    lane = lax.broadcasted_iota(jnp.int32, (8, 128), 1)
    for p in range(PL):
        rows_s[0, p:p + 1, :] = u_ref[R * p:R * p + 1, :]
        rows_s[1, p:p + 1, :] = u_ref[R * p + R - 1:R * p + R, :]
    kyf = ky_ref[...].astype(jnp.float32)
    to_east = jnp.zeros((8, 128), jnp.float32)
    to_west = jnp.zeros((8, 128), jnp.float32)
    for m in range(16):
        sl = slice(8 * m, 8 * m + 8)
        to_east = jnp.where(lane == m, pltpu.roll(u_ref[sl, 384:512], (m + 1) % 128, 1), to_east)
        to_east = jnp.where(lane == 16 + m, pltpu.roll(kyf[sl, 384:512], (m + 17) % 128, 1), to_east)
        to_west = jnp.where(lane == m, pltpu.roll(u_ref[sl, 0:128], m, 1) if m else u_ref[sl, 0:128], to_west)
    cols_s[0] = to_east
    cols_s[1] = to_west

    pl.semaphore_wait(barrier, 8 + NS - is_solver.astype(jnp.int32))

    def send(src, dst, i, dev):
        c = pltpu.make_async_remote_copy(src_ref=src, dst_ref=dst, send_sem=hs.at[i], recv_sem=hr.at[i],
                                         device_id=dev, device_id_type=MESH)
        c.start()
        return c

    halos = [
        send(rows_s.at[1], hrow.at[0], 0, (nxt, gy)),
        send(rows_s.at[0], hrow.at[1], 1, (prev, gy)),
        send(cols_s.at[0], hcol.at[0], 2, (me, east)),
        send(cols_s.at[1], hcol.at[1], 3, (me, west)),
        send(rows_s.at[1, :, pl.ds(384, 128)], hcor.at[0], 4, (nxt, east)),
        send(rows_s.at[1, :, pl.ds(0, 128)], hcor.at[1], 5, (nxt, west)),
        send(rows_s.at[0, :, pl.ds(384, 128)], hcor.at[2], 6, (prev, east)),
        send(rows_s.at[0, :, pl.ds(0, 128)], hcor.at[3], 7, (prev, west)),
    ]

    loads[2].wait()
    ik = 1.0 / kx_ref[...].astype(jnp.float32)
    for q in range(NS):
        ik_s[128 * q:128 * q + 128, :] = ik[:, 128 * q:128 * q + 128]
    a = d = jnp.ones((16, 128), jnp.float32)
    b = c = jnp.zeros((16, 128), jnp.float32)
    for i in range(R):
        row = pl.ds(i, 16, stride=R)
        a_s[row, :] = a
        b_s[row, :] = b
        ik = ik_s[row, :]
        c = c + a
        a = a + c * ik
        d = d + b
        b = b + d * ik

    def put(k, value):
        for q in range(NS):
            msg[q, 4 * k:4 * k + 4, :] = value[4 * q:4 * q + 4, :]

    for k, value in enumerate((a, b, c, d)):
        put(k, value)

    loads[3].wait()
    for h in halos:
        h.wait()

    lane_w = lax.broadcasted_iota(jnp.int32, (R, W), 1)
    row_w = lax.broadcasted_iota(jnp.int32, (R, W), 0)
    lane_p = lax.broadcasted_iota(jnp.int32, (PL, W), 1)
    col_w = jnp.where(gy == 0, 0.0, hcol[0])
    col_e = jnp.where(gy == 7, 0.0, hcol[1])

    def wide(tile, at_end):
        rest = jnp.zeros((tile.shape[0], W - 128), jnp.float32)
        return jnp.concatenate([rest, tile] if at_end else [tile, rest], axis=1)

    def halo_diff(row, cor_w, cor_e, missing):
        cw = jnp.where(gy == 0, 0.0, cor_w)
        ce = jnp.where(gy == 7, 0.0, cor_e)
        w = jnp.where(lane_p == 0, wide(pltpu.roll(cw, 1, 1), False), pltpu.roll(row, 1, 1))
        e = jnp.where(lane_p == W - 1, wide(pltpu.roll(ce, 127, 1), True), pltpu.roll(row, W - 1, 1))
        return jnp.where(missing, 0.0, e - w)

    d_prev = halo_diff(hrow[0], hcor[0], hcor[1], me == 0)
    d_next = halo_diff(hrow[1], hcor[2], hcor[3], me == NB - 1)

    for p in range(PL):
        sl = slice(R * p, R * p + R)
        u = u_ref[sl, :]
        ky = ky_ref[sl, :].astype(jnp.float32)
        g = g_ref[sl, :].astype(jnp.float32)
        cw, ck, ce = [], [], []
        for q in range(4):
            m = 4 * p + q
            cw.append(pltpu.roll(col_w, 128 - m, 1) if m else col_w)
            ck.append(pltpu.roll(col_w, 112 - m, 1))
            ce.append(pltpu.roll(col_e, 127 - m, 1))
        cw, ck, ce = (jnp.concatenate(t, axis=0) for t in (cw, ck, ce))
        uw = jnp.where(lane_w == 0, wide(cw, False), pltpu.roll(u, 1, 1))
        kb = jnp.where(lane_w == 0, wide(ck, False), pltpu.roll(ky, 1, 1))
        ue = jnp.where(lane_w == W - 1, wide(ce, True), pltpu.roll(u, W - 1, 1))
        dd = ue - uw
        up = jnp.where(row_w == 0, d_prev[p:p + 1, :], pltpu.roll(dd, 1, 0))
        dn = jnp.where(row_w == R - 1, d_next[p:p + 1, :], pltpu.roll(dd, R - 1, 0))
        right = u + (ky * (ue - u) - kb * (u - uw)) + g * (dn - up) * 0.25
        r_ref[sl, :] = right
        for q in range(NS):
            r_s[128 * q + R * p:128 * q + R * p + R, :] = right[:, 128 * q:128 * q + 128]

    vx = vf = jnp.zeros((16, 128), jnp.float32)
    for i in range(R):
        row = pl.ds(i, 16, stride=R)
        v_s[row, :] = vx
        vf = vf + (vx - r_s[row, :])
        vx = vx + vf * ik_s[row, :]
    put(4, vx)
    put(5, vf)

    def map_copy(s):
        return pltpu.make_async_remote_copy(
            src_ref=msg.at[s],
            dst_ref=inbox.at[me],
            send_sem=ms.at[s], recv_sem=mr, device_id=(s, gy), device_id_type=MESH)

    for s in range(NS):
        @pl.when(me != s)
        def _():
            map_copy(s).start()

    @pl.when(is_solver)
    def _():
        for s in range(NS):
            @pl.when(me == s)
            def _():
                inbox[s] = msg[s]
        part = inbox.at[pl.ds(0, NB - 1)]
        pltpu.make_async_copy(part, part, mr).wait()

        def block(p):
            return [inbox[p, 4 * k:4 * k + 4, :] for k in range(NV)]

        groups = []
        for z in range(8):
            a, b, c, d, vx, vf = block(4 * z)
            for x in range(1, 4):
                a2, b2, c2, d2, vx2, vf2 = block(4 * z + x)
                a, c = a2 * a + b2 * c, c2 * a + d2 * c
                b, d = a2 * b + b2 * d, c2 * b + d2 * d
                vx, vf = a2 * vx + b2 * vf + vx2, c2 * vx + d2 * vf + vf2
            groups.append((a, b, c, d, vx, vf))
        zero = jnp.zeros((PL, 128), jnp.float32)
        left = [(zero, zero)]
        for z in range(7):
            a, b, c, d, vx, vf = groups[z]
            gl, jl = left[-1]
            inv = 1.0 / (a + b * gl)
            gn = (c + d * gl) * inv
            left.append((gn, jl * inv + vf - gn * vx))
        a, b, c, d, vx, vf = groups[7]
        inv = 1.0 / b
        right = [(a * inv, -vx * inv)]
        for z in range(6, -1, -1):
            a, b, c, d, vx, vf = groups[z]
            gr, jr = right[0]
            inv = 1.0 / (d + gr * b)
            right.insert(0, ((c + gr * a) * inv, (jr - vf - gr * vx) * inv))
        for z in range(8):
            gl, jl = left[z]
            gr, jr = right[z]
            x0 = (jr - jl) / (gl + gr)
            f0 = gl * x0 + jl
            for x in range(4):
                p = 4 * z + x
                res[p, 0:4, :] = x0
                res[p, 4:8, :] = f0
                if x < 3:
                    a, b, c, d, vx, vf = block(p)
                    x0, f0 = a * x0 + b * f0 + vx, c * x0 + d * f0 + vf

        for k in range(1, NB):
            p = lax.rem(me + k, NS) if k < NS else k
            pltpu.make_async_remote_copy(
                src_ref=res.at[p], dst_ref=xf.at[me],
                send_sem=rs, recv_sem=rr.at[me], device_id=(p, gy), device_id_type=MESH).start()
        for s in range(NS):
            @pl.when(me == s)
            def _():
                xf[s] = res[s]

    for s in range(NS):
        @pl.when(me != s)
        def _():
            pltpu.make_async_copy(xf.at[s], xf.at[s], rr.at[s]).wait()

    for s in range(NS):
        @pl.when(me != s)
        def _():
            map_copy(s).wait_send()

    @pl.when(is_solver)
    def _():
        part = res.at[pl.ds(0, NB - 1)]
        pltpu.make_async_copy(part, part, rs).wait()


def finish_kernel(r_ref, a_ref, b_ref, v_ref, xf_ref, o_hbm, r_hbm, o_ref, sems):
    right = pltpu.make_async_copy(r_ref, r_hbm, sems.at[PL])
    right.start()
    copies = []
    for p in range(PL):
        sl = slice(R * p, R * p + R)
        for s in range(NS):
            x0 = xf_ref[s, p:p + 1, :]
            f0 = xf_ref[s, 4 + p:5 + p, :]
            ts = slice(128 * s + R * p, 128 * s + R * p + R)
            o_ref[sl, 128 * s:128 * s + 128] = a_ref[ts, :] * x0 + b_ref[ts, :] * f0 + v_ref[ts, :]
        part = pl.ds(R * p, R)
        copies.append(pltpu.make_async_copy(o_ref.at[part], o_hbm.at[part], sems.at[p]))
        copies[-1].start()
    for copy in copies:
        copy.wait()
    right.wait()


def shards(state_field, x_coupling, y_coupling, cross_coeff):
    flat = (PL * R, W)
    vmem = pl.BlockSpec(memory_space=pltpu.VMEM)
    hbm = pl.BlockSpec(memory_space=pltpu.HBM)
    f32, bf16 = jnp.float32, jnp.bfloat16
    tiles = (NS * PL * R, 128)
    big = pltpu.VMEM(tiles, f32)
    dma = pltpu.SemaphoreType.DMA
    shape = jax.ShapeDtypeStruct
    args = [pltpu.with_memory_space_constraint(x.reshape(flat), pltpu.HBM)
            for x in (state_field, x_coupling, y_coupling, cross_coeff)]
    parts = pl.pallas_call(
        sweep_kernel,
        out_shape=(shape(flat, f32), shape(tiles, f32), shape(tiles, f32), shape(tiles, f32),
                   shape((NS, 8, 128), f32)),
        in_specs=[hbm] * 4,
        out_specs=(vmem,) * 5,
        scratch_shapes=[
            pltpu.VMEM(flat, f32), pltpu.VMEM(flat, bf16), pltpu.VMEM(flat, bf16), pltpu.VMEM(flat, bf16),
            pltpu.VMEM((2, PL, W), f32), pltpu.VMEM((2, 8, 128), f32),
            pltpu.VMEM((2, PL, W), f32), pltpu.VMEM((2, 8, 128), f32), pltpu.VMEM((4, PL, 128), f32),
            big, big,
            pltpu.VMEM((NS, PL * NV, 128), f32), pltpu.VMEM((NB, PL * NV, 128), f32),
            pltpu.VMEM((NB, 8, 128), f32),
            dma((4,)), dma((8,)), dma((8,)), dma((NS,)), dma(()), dma(()), dma((NS,)),
        ],
        compiler_params=pltpu.CompilerParams(
            collective_id=0, has_side_effects=True, vmem_limit_bytes=32 * 2**20),
    )(*args)
    out, rhs = pl.pallas_call(
        finish_kernel,
        out_shape=(shape(flat, f32),) * 2,
        in_specs=[vmem] * 5,
        out_specs=(hbm, hbm),
        scratch_shapes=[pltpu.VMEM(flat, f32), dma((PL + 1,))],
        compiler_params=pltpu.CompilerParams(vmem_limit_bytes=32 * 2**20),
    )(*parts)
    return out.reshape(state_field.shape), rhs.reshape(state_field.shape)


def solution(mesh):
    spec = P(None, "gx", "gy")
    return jax.shard_map(shards, mesh=mesh, in_specs=(spec,) * 4, out_specs=(spec, spec), check_vma=False)
```

```python
import jax
import jax.numpy as jnp
from jax import lax
from jax.experimental import pallas as pl
from jax.experimental.pallas import tpu as pltpu
from jax.sharding import PartitionSpec as P

MESH = pl.DeviceIdType.MESH
PL = 4
R = 32
W = 512
NB = 32
NQ = 4
START = 0
NS = 8
PG = 16 // NS
NV = 6


def sweep_kernel(u_hbm, kx_hbm, ky_hbm, g_hbm, r_ref, a_s, b_s, v_s, xf, shift,
                 u_ref, kx_ref, ky_ref, g_ref,
                 rows_s, cols_s, hrow, hcol, hcor, es,
                 ik_s, r_s, msg, inbox, res,
                 ls, hs, hr, ms, mr, rs, rr):
    loads = [pltpu.make_async_copy(src, dst, ls.at[i]) for i, (src, dst) in enumerate(
        ((u_hbm, u_ref), (ky_hbm, ky_ref), (kx_hbm, kx_ref), (g_hbm, g_ref)))]
    for load in loads:
        load.start()
    me = lax.axis_index("gx")
    gy = lax.axis_index("gy")
    prev, nxt = lax.rem(me + NB - 1, NB), lax.rem(me + 1, NB)
    west, east = lax.rem(gy + 7, 8), lax.rem(gy + 1, 8)

    def signal(dev):
        pl.semaphore_signal(barrier, inc=1, device_id=dev, device_id_type=MESH)

    barrier = pltpu.get_barrier_semaphore()
    slot = lax.rem(me + NB - START, NB)
    is_solver = slot < NS

    @pl.when(is_solver)
    def _():
        for k in range(1, NB):
            signal((lax.rem(me + k, NB), gy))

    for dev in ((prev, gy), (nxt, gy), (me, west), (me, east)):
        signal(dev)

    loads[0].wait()
    loads[1].wait()

    lane = lax.broadcasted_iota(jnp.int32, (8, 128), 1)
    for p in range(PL):
        rows_s[0, p:p + 1, :] = u_ref[R * p:R * p + 1, :]
        rows_s[1, p:p + 1, :] = u_ref[R * p + R - 1:R * p + R, :]
    kyf = ky_ref[...].astype(jnp.float32)
    to_east = jnp.zeros((8, 128), jnp.float32)
    to_west = jnp.zeros((8, 128), jnp.float32)
    for m in range(16):
        sl = slice(8 * m, 8 * m + 8)
        to_east = jnp.where(lane == m, pltpu.roll(u_ref[sl, 384:512], (m + 1) % 128, 1), to_east)
        to_east = jnp.where(lane == 16 + m, pltpu.roll(kyf[sl, 384:512], (m + 17) % 128, 1), to_east)
        to_west = jnp.where(lane == m, pltpu.roll(u_ref[sl, 0:128], m, 1) if m else u_ref[sl, 0:128], to_west)
    cols_s[0] = to_east
    cols_s[1] = to_west

    pl.semaphore_wait(barrier, 4 + NS - is_solver.astype(jnp.int32))

    def send(src, dst, i, dev):
        c = pltpu.make_async_remote_copy(src_ref=src, dst_ref=dst, send_sem=hs.at[i], recv_sem=hr.at[i],
                                         device_id=dev, device_id_type=MESH)
        c.start()
        return c

    halos = [
        send(rows_s.at[1], hrow.at[0], 0, (nxt, gy)),
        send(rows_s.at[0], hrow.at[1], 1, (prev, gy)),
        send(cols_s.at[0], hcol.at[0], 2, (me, east)),
        send(cols_s.at[1], hcol.at[1], 3, (me, west)),
    ]

    loads[2].wait()
    ik = 1.0 / kx_ref[...].astype(jnp.float32)
    for q in range(NQ):
        ik_s[128 * q:128 * q + 128, :] = ik[:, 128 * q:128 * q + 128]
    a = d = jnp.ones((16, 128), jnp.float32)
    b = c = jnp.zeros((16, 128), jnp.float32)
    for i in range(R):
        row = pl.ds(i, 16, stride=R)
        a_s[row, :] = a
        b_s[row, :] = b
        ik = ik_s[row, :]
        c = c + a
        a = a + c * ik
        d = d + b
        b = b + d * ik

    def put(k, value):
        for s in range(NS):
            msg[s, PG * k:PG * k + PG, :] = value[PG * s:PG * s + PG, :]

    for k, value in enumerate((a, b, c)):
        put(k, value)
    es[...] = jnp.zeros((6, 16, 128), jnp.float32)

    loads[3].wait()
    for h in halos:
        h.wait()

    lane_w = lax.broadcasted_iota(jnp.int32, (R, W), 1)
    row_w = lax.broadcasted_iota(jnp.int32, (R, W), 0)
    lane_p = lax.broadcasted_iota(jnp.int32, (PL, W), 1)
    col_w = jnp.where(gy == 0, 0.0, hcol[0])
    col_e = jnp.where(gy == 7, 0.0, hcol[1])

    def wide(tile, at_end):
        rest = jnp.zeros((tile.shape[0], W - 128), jnp.float32)
        return jnp.concatenate([rest, tile] if at_end else [tile, rest], axis=1)

    def halo_diff(row, missing):
        w = jnp.where(lane_p == 0, 0.0, pltpu.roll(row, 1, 1))
        e = jnp.where(lane_p == W - 1, 0.0, pltpu.roll(row, W - 1, 1))
        return jnp.where(missing, 0.0, e - w)

    d_prev = halo_diff(hrow[0], me == 0)
    d_next = halo_diff(hrow[1], me == NB - 1)

    for p in range(PL):
        sl = slice(R * p, R * p + R)
        u = u_ref[sl, :]
        ky = ky_ref[sl, :].astype(jnp.float32)
        g = g_ref[sl, :].astype(jnp.float32)
        cw, ck, ce = [], [], []
        for q in range(4):
            m = 4 * p + q
            cw.append(pltpu.roll(col_w, 128 - m, 1) if m else col_w)
            ck.append(pltpu.roll(col_w, 112 - m, 1))
            ce.append(pltpu.roll(col_e, 127 - m, 1))
        cw, ck, ce = (jnp.concatenate(t, axis=0) for t in (cw, ck, ce))
        for k, row in ((0, 0), (1, R - 1)):
            es[k, p:p + 1, :] = -cw[row:row + 1, :]
            es[k, 12 + p:13 + p, :] = ce[row:row + 1, :]
            es[2 + k, p:p + 1, :] = 0.25 * g[row:row + 1, 0:128]
            es[2 + k, 12 + p:13 + p, :] = 0.25 * g[row:row + 1, W - 128:W]
        uw = jnp.where(lane_w == 0, wide(cw, False), pltpu.roll(u, 1, 1))
        kb = jnp.where(lane_w == 0, wide(ck, False), pltpu.roll(ky, 1, 1))
        ue = jnp.where(lane_w == W - 1, wide(ce, True), pltpu.roll(u, W - 1, 1))
        dd = ue - uw
        up = jnp.where(row_w == 0, d_prev[p:p + 1, :], pltpu.roll(dd, 1, 0))
        dn = jnp.where(row_w == R - 1, d_next[p:p + 1, :], pltpu.roll(dd, R - 1, 0))
        right = u + (ky * (ue - u) - kb * (u - uw)) + g * (dn - up) * 0.25
        r_ref[sl, :] = right
        for q in range(NQ):
            r_s[128 * q + R * p:128 * q + R * p + R, :] = right[:, 128 * q:128 * q + 128]

    vx = vf = jnp.zeros((16, 128), jnp.float32)
    for i in range(R):
        row = pl.ds(i, 16, stride=R)
        v_s[row, :] = vx
        vf = vf + (vx - r_s[row, :])
        vx = vx + vf * ik_s[row, :]
    put(3, vx)
    put(4, vf)

    lane_t = lax.broadcasted_iota(jnp.int32, (16, 128), 1)
    tile_t = lax.broadcasted_iota(jnp.int32, (16, 128), 0) // PL

    def at_edge(k):
        return ((tile_t == 0) & (lane_t == k)) | ((tile_t == NQ - 1) & (lane_t == (127 + k) % 128))

    edge = jnp.zeros((16, 128), jnp.float32)
    for k, value in enumerate((es[0], es[1], es[2], es[3], ik_s[pl.ds(R - 1, 16, stride=R), :])):
        edge = jnp.where(at_edge(k), pltpu.roll(value, k, 1) if k else value, edge)
    put(5, edge)

    def map_copy(s):
        return pltpu.make_async_remote_copy(
            src_ref=msg.at[s],
            dst_ref=inbox.at[me],
            send_sem=ms.at[s], recv_sem=mr, device_id=((START + s) % NB, gy), device_id_type=MESH)

    for s in range(NS):
        @pl.when(slot != s)
        def _():
            map_copy(s).start()

    corners = [send(hcol, hcor.at[0], 4, (nxt, gy)), send(hcol, hcor.at[1], 5, (prev, gy))]

    @pl.when(is_solver)
    def _():
        for s in range(NS):
            @pl.when(slot == s)
            def _():
                inbox[(START + s) % NB] = msg[s]
        part = inbox.at[pl.ds(0, NB - 1)]
        pltpu.make_async_copy(part, part, mr).wait()

        def block(p):
            a, b, c, vx, vf = (inbox[p, PG * k:PG * k + PG, :] for k in range(NV - 1))
            return a, b, c, (1.0 + b * c) / a, vx, vf

        tile = slot * PG // PL
        line = jnp.where(tile == 0, 0, jnp.where(tile == NQ - 1, 127, -1))

        @pl.when(line >= 0)
        def _():
            here = lax.broadcasted_iota(jnp.int32, (PG, 128), 1) == line

            def edges(p):
                e = inbox[p, PG * (NV - 1):PG * NV, :]
                return [e] + [pltpu.roll(e, 128 - k, 1) for k in range(1, 5)]

            before, own = None, edges(0)
            for p in range(NB):
                after = edges(p + 1) if p < NB - 1 else None
                a, b, c, d, vx, vf = block(p)
                if before is not None:
                    first = own[2] * before[1]
                    vx, vf = vx + b * first, vf + d * first
                if after is not None:
                    last = own[3] * after[0]
                    vx, vf = vx - own[4] * last, vf - last
                inbox[p, PG * 3:PG * 4, :] = jnp.where(here, vx, inbox[p, PG * 3:PG * 4, :])
                inbox[p, PG * 4:PG * 5, :] = jnp.where(here, vf, inbox[p, PG * 4:PG * 5, :])
                before, own = own, after

        groups = []
        for z in range(8):
            a, b, c, d, vx, vf = block(4 * z)
            for x in range(1, 4):
                a2, b2, c2, d2, vx2, vf2 = block(4 * z + x)
                a, c = a2 * a + b2 * c, c2 * a + d2 * c
                b, d = a2 * b + b2 * d, c2 * b + d2 * d
                vx, vf = a2 * vx + b2 * vf + vx2, c2 * vx + d2 * vf + vf2
            groups.append((a, b, c, d, vx, vf))
        zero = jnp.zeros((PG, 128), jnp.float32)
        left = [(zero, zero)]
        for z in range(7):
            a, b, c, d, vx, vf = groups[z]
            gl, jl = left[-1]
            inv = 1.0 / (a + b * gl)
            gn = (c + d * gl) * inv
            left.append((gn, jl * inv + vf - gn * vx))
        a, b, c, d, vx, vf = groups[7]
        inv = 1.0 / b
        right = [(a * inv, -vx * inv)]
        for z in range(6, -1, -1):
            a, b, c, d, vx, vf = groups[z]
            gr, jr = right[0]
            inv = 1.0 / (d + gr * b)
            right.insert(0, ((c + gr * a) * inv, (jr - vf - gr * vx) * inv))
        for z in range(8):
            gl, jl = left[z]
            gr, jr = right[z]
            x0 = (jr - jl) / (gl + gr)
            f0 = gl * x0 + jl
            for x in range(4):
                p = 4 * z + x
                res[p, 0:PG, :] = x0
                res[p, PG:2 * PG, :] = f0
                if x < 3:
                    a, b, c, d, vx, vf = block(p)
                    x0, f0 = a * x0 + b * f0 + vx, c * x0 + d * f0 + vf

        for p in range(NB):
            @pl.when(me != p)
            def _():
                pltpu.make_async_remote_copy(
                    src_ref=res.at[p], dst_ref=xf.at[slot],
                    send_sem=rs, recv_sem=rr.at[slot], device_id=(p, gy), device_id_type=MESH).start()
        for s in range(NS):
            @pl.when(slot == s)
            def _():
                xf[s] = res[(START + s) % NB]

    for corner in corners:
        corner.wait()
    for p in range(PL):
        for k, missing, row, m in ((4, me == 0, 7, 4 * p + 3), (5, me == NB - 1, 0, 4 * p)):
            w = pltpu.roll(hcor[k - 4, 0], 128 - m, 1) if m else hcor[k - 4, 0]
            e = pltpu.roll(hcor[k - 4, 1], 127 - m, 1)
            es[k, p:p + 1, :] = jnp.where(missing | (gy == 0), 0.0, -w[row:row + 1, :])
            es[k, 12 + p:13 + p, :] = jnp.where(missing | (gy == 7), 0.0, e[row:row + 1, :])
    first = jnp.where(at_edge(0), -es[2] * es[4], 0.0)
    last = jnp.where(at_edge(0), es[3] * es[5], 0.0)
    shift[...] = first
    for p in range(PL):
        for q in (0, NQ - 1):
            ls_q, t = slice(128 * q, 128 * q + 128), PL * q + p
            r_ref[R * p:R * p + 1, ls_q] = r_ref[R * p:R * p + 1, ls_q] + first[t:t + 1, :]
            r_ref[R * p + R - 1:R * p + R, ls_q] = r_ref[R * p + R - 1:R * p + R, ls_q] + last[t:t + 1, :]

    for s in range(NS):
        @pl.when(slot != s)
        def _():
            pltpu.make_async_copy(xf.at[s], xf.at[s], rr.at[s]).wait()

    for s in range(NS):
        @pl.when(slot != s)
        def _():
            map_copy(s).wait_send()

    @pl.when(is_solver)
    def _():
        part = res.at[pl.ds(0, NB - 1)]
        pltpu.make_async_copy(part, part, rs).wait()


def finish_kernel(r_ref, a_ref, b_ref, v_ref, xf_ref, shift_ref, o_hbm, r_hbm, o_ref, sems):
    right = pltpu.make_async_copy(r_ref, r_hbm, sems.at[PL])
    right.start()
    copies = []
    for p in range(PL):
        sl = slice(R * p, R * p + R)
        for q in range(NQ):
            s, h = divmod(PL * q + p, PG)
            x0 = xf_ref[s, h:h + 1, :]
            f0 = xf_ref[s, PG + h:PG + h + 1, :] - shift_ref[PL * q + p:PL * q + p + 1, :]
            ts = slice(128 * q + R * p, 128 * q + R * p + R)
            o_ref[sl, 128 * q:128 * q + 128] = a_ref[ts, :] * x0 + b_ref[ts, :] * f0 + v_ref[ts, :]
        part = pl.ds(R * p, R)
        copies.append(pltpu.make_async_copy(o_ref.at[part], o_hbm.at[part], sems.at[p]))
        copies[-1].start()
    for copy in copies:
        copy.wait()
    right.wait()


def shards(state_field, x_coupling, y_coupling, cross_coeff):
    flat = (PL * R, W)
    vmem = pl.BlockSpec(memory_space=pltpu.VMEM)
    hbm = pl.BlockSpec(memory_space=pltpu.HBM)
    f32, bf16 = jnp.float32, jnp.bfloat16
    tiles = (NQ * PL * R, 128)
    big = pltpu.VMEM(tiles, f32)
    dma = pltpu.SemaphoreType.DMA
    shape = jax.ShapeDtypeStruct
    args = [pltpu.with_memory_space_constraint(x.reshape(flat), pltpu.HBM)
            for x in (state_field, x_coupling, y_coupling, cross_coeff)]
    parts = pl.pallas_call(
        sweep_kernel,
        out_shape=(shape(flat, f32), shape(tiles, f32), shape(tiles, f32), shape(tiles, f32),
                   shape((NS, 2 * PG, 128), f32), shape((16, 128), f32)),
        in_specs=[hbm] * 4,
        out_specs=(vmem,) * 6,
        scratch_shapes=[
            pltpu.VMEM(flat, f32), pltpu.VMEM(flat, bf16), pltpu.VMEM(flat, bf16), pltpu.VMEM(flat, bf16),
            pltpu.VMEM((2, PL, W), f32), pltpu.VMEM((2, 8, 128), f32),
            pltpu.VMEM((2, PL, W), f32), pltpu.VMEM((2, 8, 128), f32), pltpu.VMEM((2, 2, 8, 128), f32),
            pltpu.VMEM((6, 16, 128), f32),
            big, big,
            pltpu.VMEM((NS, PG * NV, 128), f32), pltpu.VMEM((NB, PG * NV, 128), f32),
            pltpu.VMEM((NB, 2 * PG, 128), f32),
            dma((4,)), dma((6,)), dma((6,)), dma((NS,)), dma(()), dma(()), dma((NS,)),
        ],
        compiler_params=pltpu.CompilerParams(
            collective_id=0, has_side_effects=True, vmem_limit_bytes=32 * 2**20),
    )(*args)
    out, rhs = pl.pallas_call(
        finish_kernel,
        out_shape=(shape(flat, f32),) * 2,
        in_specs=[vmem] * 6,
        out_specs=(hbm, hbm),
        scratch_shapes=[pltpu.VMEM(flat, f32), dma((PL + 1,))],
        compiler_params=pltpu.CompilerParams(vmem_limit_bytes=32 * 2**20),
    )(*parts)
    return out.reshape(state_field.shape), rhs.reshape(state_field.shape)


def solution(mesh):
    spec = P(None, "gx", "gy")
    return jax.shard_map(shards, mesh=mesh, in_specs=(spec,) * 4, out_specs=(spec, spec), check_vma=False)
```

```python
import jax
import jax.numpy as jnp
from jax import lax
from jax.experimental import pallas as pl
from jax.experimental.pallas import tpu as pltpu
from jax.sharding import PartitionSpec as P

MESH = pl.DeviceIdType.MESH
PL = 4
R = 32
W = 512
NB = 32
NQ = 4
START = 0
NS = 4
PG = 16 // NS
NV = 3


def sweep_kernel(u_hbm, kx_hbm, ky_hbm, g_hbm, r_ref, a_s, b_s, v_s, xf, shift,
                 u_ref, kx_ref, ky_ref, g_ref,
                 rows_s, cols_s, hrow, hcol, hcor, es,
                 ik_s, r_s, msg, inbox, dmat, gmat, res,
                 ls, hs, hr, ms, mr, rs, rr):
    loads = [pltpu.make_async_copy(src, dst, ls.at[i]) for i, (src, dst) in enumerate(
        ((u_hbm, u_ref), (ky_hbm, ky_ref), (kx_hbm, kx_ref), (g_hbm, g_ref)))]
    for load in loads:
        load.start()
    me = lax.axis_index("gx")
    gy = lax.axis_index("gy")
    prev, nxt = lax.rem(me + NB - 1, NB), lax.rem(me + 1, NB)
    west, east = lax.rem(gy + 7, 8), lax.rem(gy + 1, 8)

    def signal(dev):
        pl.semaphore_signal(barrier, inc=1, device_id=dev, device_id_type=MESH)

    barrier = pltpu.get_barrier_semaphore()
    slot = lax.rem(me + NB - START, NB)
    is_solver = slot < NS

    @pl.when(is_solver)
    def _():
        for k in range(1, NB):
            signal((lax.rem(me + k, NB), gy))

    for dev in ((prev, gy), (nxt, gy), (me, west), (me, east)):
        signal(dev)

    loads[0].wait()
    loads[1].wait()

    lane = lax.broadcasted_iota(jnp.int32, (8, 128), 1)
    for p in range(PL):
        rows_s[0, p:p + 1, :] = u_ref[R * p:R * p + 1, :]
        rows_s[1, p:p + 1, :] = u_ref[R * p + R - 1:R * p + R, :]
    kyf = ky_ref[...].astype(jnp.float32)
    to_east = jnp.zeros((8, 128), jnp.float32)
    to_west = jnp.zeros((8, 128), jnp.float32)
    for m in range(16):
        sl = slice(8 * m, 8 * m + 8)
        to_east = jnp.where(lane == m, pltpu.roll(u_ref[sl, 384:512], (m + 1) % 128, 1), to_east)
        to_east = jnp.where(lane == 16 + m, pltpu.roll(kyf[sl, 384:512], (m + 17) % 128, 1), to_east)
        to_west = jnp.where(lane == m, pltpu.roll(u_ref[sl, 0:128], m, 1) if m else u_ref[sl, 0:128], to_west)
    cols_s[0] = to_east
    cols_s[1] = to_west

    pl.semaphore_wait(barrier, 4 + NS - is_solver.astype(jnp.int32))

    def send(src, dst, i, dev):
        c = pltpu.make_async_remote_copy(src_ref=src, dst_ref=dst, send_sem=hs.at[i], recv_sem=hr.at[i],
                                         device_id=dev, device_id_type=MESH)
        c.start()
        return c

    halos = [
        send(rows_s.at[1], hrow.at[0], 0, (nxt, gy)),
        send(rows_s.at[0], hrow.at[1], 1, (prev, gy)),
        send(cols_s.at[0], hcol.at[0], 2, (me, east)),
        send(cols_s.at[1], hcol.at[1], 3, (me, west)),
    ]

    loads[2].wait()
    ik = 1.0 / kx_ref[...].astype(jnp.float32)
    for q in range(NQ):
        ik_s[128 * q:128 * q + 128, :] = ik[:, 128 * q:128 * q + 128]
    a = d = jnp.ones((16, 128), jnp.float32)
    b = c = jnp.zeros((16, 128), jnp.float32)
    for i in range(R):
        row = pl.ds(i, 16, stride=R)
        a_s[row, :] = a
        b_s[row, :] = b
        ik = ik_s[row, :]
        c = c + a
        a = a + c * ik
        d = d + b
        b = b + d * ik

    def put(half, k, value):
        for s in range(NS):
            msg[half, s, PG * k:PG * k + PG, :] = value[PG * s:PG * s + PG, :]

    def on_edge(s):
        return PG * s // PL in (0, NQ - 1)

    def map_copy(half, s):
        rows = pl.ds(0, PG * (NV if half == 0 or on_edge(s) else NV - 1))
        return pltpu.make_async_remote_copy(
            src_ref=msg.at[half, s, rows],
            dst_ref=inbox.at[half, me, rows],
            send_sem=ms.at[half, s], recv_sem=mr.at[half], device_id=((START + s) % NB, gy), device_id_type=MESH)

    def send_maps(half):
        for s in range(NS):
            @pl.when(slot != s)
            def _():
                map_copy(half, s).start()

            @pl.when(slot == s)
            def _():
                inbox[half, (START + s) % NB] = msg[half, s]

    for k, value in enumerate((a, b, c)):
        put(0, k, value)
    send_maps(0)
    es[...] = jnp.zeros((6, 16, 128), jnp.float32)

    loads[3].wait()
    for h in halos:
        h.wait()

    lane_w = lax.broadcasted_iota(jnp.int32, (R, W), 1)
    row_w = lax.broadcasted_iota(jnp.int32, (R, W), 0)
    lane_p = lax.broadcasted_iota(jnp.int32, (PL, W), 1)
    col_w = jnp.where(gy == 0, 0.0, hcol[0])
    col_e = jnp.where(gy == 7, 0.0, hcol[1])

    def wide(tile, at_end):
        rest = jnp.zeros((tile.shape[0], W - 128), jnp.float32)
        return jnp.concatenate([rest, tile] if at_end else [tile, rest], axis=1)

    def halo_diff(row, missing):
        w = jnp.where(lane_p == 0, 0.0, pltpu.roll(row, 1, 1))
        e = jnp.where(lane_p == W - 1, 0.0, pltpu.roll(row, W - 1, 1))
        return jnp.where(missing, 0.0, e - w)

    d_prev = halo_diff(hrow[0], me == 0)
    d_next = halo_diff(hrow[1], me == NB - 1)

    for p in range(PL):
        sl = slice(R * p, R * p + R)
        u = u_ref[sl, :]
        ky = ky_ref[sl, :].astype(jnp.float32)
        g = g_ref[sl, :].astype(jnp.float32)
        cw, ck, ce = [], [], []
        for q in range(4):
            m = 4 * p + q
            cw.append(pltpu.roll(col_w, 128 - m, 1) if m else col_w)
            ck.append(pltpu.roll(col_w, 112 - m, 1))
            ce.append(pltpu.roll(col_e, 127 - m, 1))
        cw, ck, ce = (jnp.concatenate(t, axis=0) for t in (cw, ck, ce))
        for k, row in ((0, 0), (1, R - 1)):
            es[k, p:p + 1, :] = -cw[row:row + 1, :]
            es[k, 12 + p:13 + p, :] = ce[row:row + 1, :]
            es[2 + k, p:p + 1, :] = 0.25 * g[row:row + 1, 0:128]
            es[2 + k, 12 + p:13 + p, :] = 0.25 * g[row:row + 1, W - 128:W]
        uw = jnp.where(lane_w == 0, wide(cw, False), pltpu.roll(u, 1, 1))
        kb = jnp.where(lane_w == 0, wide(ck, False), pltpu.roll(ky, 1, 1))
        ue = jnp.where(lane_w == W - 1, wide(ce, True), pltpu.roll(u, W - 1, 1))
        dd = ue - uw
        up = jnp.where(row_w == 0, d_prev[p:p + 1, :], pltpu.roll(dd, 1, 0))
        dn = jnp.where(row_w == R - 1, d_next[p:p + 1, :], pltpu.roll(dd, R - 1, 0))
        right = u + (ky * (ue - u) - kb * (u - uw)) + g * (dn - up) * 0.25
        r_ref[sl, :] = right
        for q in range(NQ):
            r_s[128 * q + R * p:128 * q + R * p + R, :] = right[:, 128 * q:128 * q + 128]

    vx = vf = jnp.zeros((16, 128), jnp.float32)
    for i in range(R):
        row = pl.ds(i, 16, stride=R)
        v_s[row, :] = vx
        vf = vf + (vx - r_s[row, :])
        vx = vx + vf * ik_s[row, :]
    put(1, 0, vx)
    put(1, 1, vf)

    lane_t = lax.broadcasted_iota(jnp.int32, (16, 128), 1)
    tile_t = lax.broadcasted_iota(jnp.int32, (16, 128), 0) // PL

    def at_edge(k):
        return ((tile_t == 0) & (lane_t == k)) | ((tile_t == NQ - 1) & (lane_t == (127 + k) % 128))

    edge = jnp.zeros((16, 128), jnp.float32)
    for k, value in enumerate((es[0], es[1], es[2], es[3], ik_s[pl.ds(R - 1, 16, stride=R), :])):
        edge = jnp.where(at_edge(k), pltpu.roll(value, k, 1) if k else value, edge)
    put(1, 2, edge)
    send_maps(1)

    corners = [send(hcol, hcor.at[0], 4, (nxt, gy)), send(hcol, hcor.at[1], 5, (prev, gy))]

    @pl.when(is_solver)
    def _():
        def arrived(half, count):
            part = inbox.at[half, pl.ds(0, NB - 1), pl.ds(0, PG * count)]
            pltpu.make_async_copy(part, part, mr.at[half]).wait()

        def matrix(p):
            a, b, c = (inbox[0, p, PG * k:PG * k + PG, :] for k in range(3))
            return a, b, c, (1.0 + b * c) / a

        def offset(p):
            return [inbox[1, p, PG * k:PG * k + PG, :] for k in range(2)]

        arrived(0, NV)
        groups = []
        for z in range(8):
            a, b, c, d = matrix(4 * z)
            dmat[4 * z] = d
            for x in range(1, 4):
                a2, b2, c2, d2 = matrix(4 * z + x)
                dmat[4 * z + x] = d2
                a, c = a2 * a + b2 * c, c2 * a + d2 * c
                b, d = a2 * b + b2 * d, c2 * b + d2 * d
            groups.append((a, b, c, d))
        zero = jnp.zeros((PG, 128), jnp.float32)
        gl, gr = zero, zero
        gls, grs, invl, invr = [zero], [], [], []
        for z in range(7):
            a, b, c, d = groups[z]
            invl.append(1.0 / (a + b * gl))
            gl = (c + d * gl) * invl[-1]
            gls.append(gl)
        a, b, c, d = groups[7]
        invr.append(1.0 / b)
        gr = a * invr[0]
        grs.append(gr)
        for z in range(6, -1, -1):
            a, b, c, d = groups[z]
            invr.insert(0, 1.0 / (d + gr * b))
            gr = (c + gr * a) * invr[0]
            grs.insert(0, gr)
        for z in range(8):
            gmat[0, z] = gls[z]
            gmat[1, z] = grs[z]
            gmat[2, z] = invl[z] if z < 7 else zero
            gmat[3, z] = invr[z]
            gmat[4, z] = 1.0 / (gls[z] + grs[z])

        tile = slot * PG // PL
        line = jnp.where(tile == 0, 0, jnp.where(tile == NQ - 1, 127, -1))

        @pl.when(line < 0)
        def _():
            arrived(1, NV - 1)

        @pl.when(line >= 0)
        def _():
            arrived(1, NV)
            here = lax.broadcasted_iota(jnp.int32, (PG, 128), 1) == line

            def edges(p):
                e = inbox[1, p, PG * (NV - 1):PG * NV, :]
                return [e] + [pltpu.roll(e, 128 - k, 1) for k in range(1, 5)]

            before, own = None, edges(0)
            for p in range(NB):
                after = edges(p + 1) if p < NB - 1 else None
                vx, vf = offset(p)
                dx = df = zero
                if before is not None:
                    first = own[2] * before[1]
                    dx, df = inbox[0, p, PG:2 * PG, :] * first, dmat[p] * first
                if after is not None:
                    last = own[3] * after[0]
                    dx, df = dx - own[4] * last, df - last
                inbox[1, p, 0:PG, :] = vx + jnp.where(here, dx, 0.0)
                inbox[1, p, PG:2 * PG, :] = vf + jnp.where(here, df, 0.0)
                before, own = own, after

        def block(p):
            a, b, c = (inbox[0, p, PG * k:PG * k + PG, :] for k in range(3))
            return a, b, c, dmat[p], *offset(p)

        sums = []
        for z in range(8):
            vx, vf = offset(4 * z)
            for x in range(1, 4):
                a2, b2, c2, d2, vx2, vf2 = block(4 * z + x)
                vx, vf = a2 * vx + b2 * vf + vx2, c2 * vx + d2 * vf + vf2
            sums.append((vx, vf))
        left, right = [zero], []
        for z in range(7):
            vx, vf = sums[z]
            left.append(left[-1] * gmat[2, z] + vf - gmat[0, z + 1] * vx)
        right.append(-sums[7][0] * gmat[3, 7])
        for z in range(6, -1, -1):
            vx, vf = sums[z]
            right.insert(0, (right[0] - vf - gmat[1, z + 1] * vx) * gmat[3, z])
        for z in range(8):
            x0 = (right[z] - left[z]) * gmat[4, z]
            f0 = gmat[0, z] * x0 + left[z]
            for x in range(4):
                p = 4 * z + x
                res[p, 0:PG, :] = x0
                res[p, PG:2 * PG, :] = f0
                if x < 3:
                    a, b, c, d, vx, vf = block(p)
                    x0, f0 = a * x0 + b * f0 + vx, c * x0 + d * f0 + vf

        for p in range(NB):
            @pl.when(me != p)
            def _():
                pltpu.make_async_remote_copy(
                    src_ref=res.at[p], dst_ref=xf.at[slot],
                    send_sem=rs, recv_sem=rr.at[slot], device_id=(p, gy), device_id_type=MESH).start()
        for s in range(NS):
            @pl.when(slot == s)
            def _():
                xf[s] = res[(START + s) % NB]

    for corner in corners:
        corner.wait()
    for p in range(PL):
        for k, missing, row, m in ((4, me == 0, 7, 4 * p + 3), (5, me == NB - 1, 0, 4 * p)):
            w = pltpu.roll(hcor[k - 4, 0], 128 - m, 1) if m else hcor[k - 4, 0]
            e = pltpu.roll(hcor[k - 4, 1], 127 - m, 1)
            es[k, p:p + 1, :] = jnp.where(missing | (gy == 0), 0.0, -w[row:row + 1, :])
            es[k, 12 + p:13 + p, :] = jnp.where(missing | (gy == 7), 0.0, e[row:row + 1, :])
    first = jnp.where(at_edge(0), -es[2] * es[4], 0.0)
    last = jnp.where(at_edge(0), es[3] * es[5], 0.0)
    shift[...] = first
    for p in range(PL):
        for q in (0, NQ - 1):
            ls_q, t = slice(128 * q, 128 * q + 128), PL * q + p
            r_ref[R * p:R * p + 1, ls_q] = r_ref[R * p:R * p + 1, ls_q] + first[t:t + 1, :]
            r_ref[R * p + R - 1:R * p + R, ls_q] = r_ref[R * p + R - 1:R * p + R, ls_q] + last[t:t + 1, :]

    for s in range(NS):
        @pl.when(slot != s)
        def _():
            pltpu.make_async_copy(xf.at[s], xf.at[s], rr.at[s]).wait()

    for s in range(NS):
        @pl.when(slot != s)
        def _():
            map_copy(0, s).wait_send()
            map_copy(1, s).wait_send()

    @pl.when(is_solver)
    def _():
        part = res.at[pl.ds(0, NB - 1)]
        pltpu.make_async_copy(part, part, rs).wait()


def finish_kernel(r_ref, a_ref, b_ref, v_ref, xf_ref, shift_ref, o_hbm, r_hbm, o_ref, sems):
    right = pltpu.make_async_copy(r_ref, r_hbm, sems.at[PL])
    right.start()
    copies = []
    for p in range(PL):
        sl = slice(R * p, R * p + R)
        for q in range(NQ):
            s, h = divmod(PL * q + p, PG)
            x0 = xf_ref[s, h:h + 1, :]
            f0 = xf_ref[s, PG + h:PG + h + 1, :] - shift_ref[PL * q + p:PL * q + p + 1, :]
            ts = slice(128 * q + R * p, 128 * q + R * p + R)
            o_ref[sl, 128 * q:128 * q + 128] = a_ref[ts, :] * x0 + b_ref[ts, :] * f0 + v_ref[ts, :]
        part = pl.ds(R * p, R)
        copies.append(pltpu.make_async_copy(o_ref.at[part], o_hbm.at[part], sems.at[p]))
        copies[-1].start()
    for copy in copies:
        copy.wait()
    right.wait()


def shards(state_field, x_coupling, y_coupling, cross_coeff):
    flat = (PL * R, W)
    vmem = pl.BlockSpec(memory_space=pltpu.VMEM)
    hbm = pl.BlockSpec(memory_space=pltpu.HBM)
    f32, bf16 = jnp.float32, jnp.bfloat16
    tiles = (NQ * PL * R, 128)
    big = pltpu.VMEM(tiles, f32)
    dma = pltpu.SemaphoreType.DMA
    shape = jax.ShapeDtypeStruct
    args = [pltpu.with_memory_space_constraint(x.reshape(flat), pltpu.HBM)
            for x in (state_field, x_coupling, y_coupling, cross_coeff)]
    parts = pl.pallas_call(
        sweep_kernel,
        out_shape=(shape(flat, f32), shape(tiles, f32), shape(tiles, f32), shape(tiles, f32),
                   shape((NS, 2 * PG, 128), f32), shape((16, 128), f32)),
        in_specs=[hbm] * 4,
        out_specs=(vmem,) * 6,
        scratch_shapes=[
            pltpu.VMEM(flat, f32), pltpu.VMEM(flat, bf16), pltpu.VMEM(flat, bf16), pltpu.VMEM(flat, bf16),
            pltpu.VMEM((2, PL, W), f32), pltpu.VMEM((2, 8, 128), f32),
            pltpu.VMEM((2, PL, W), f32), pltpu.VMEM((2, 8, 128), f32), pltpu.VMEM((2, 2, 8, 128), f32),
            pltpu.VMEM((6, 16, 128), f32),
            big, big,
            pltpu.VMEM((2, NS, PG * NV, 128), f32), pltpu.VMEM((2, NB, PG * NV, 128), f32),
            pltpu.VMEM((NB, PG, 128), f32), pltpu.VMEM((5, 8, PG, 128), f32),
            pltpu.VMEM((NB, 2 * PG, 128), f32),
            dma((4,)), dma((6,)), dma((6,)), dma((2, NS)), dma((2,)), dma(()), dma((NS,)),
        ],
        compiler_params=pltpu.CompilerParams(
            collective_id=0, has_side_effects=True, vmem_limit_bytes=32 * 2**20),
    )(*args)
    out, rhs = pl.pallas_call(
        finish_kernel,
        out_shape=(shape(flat, f32),) * 2,
        in_specs=[vmem] * 6,
        out_specs=(hbm, hbm),
        scratch_shapes=[pltpu.VMEM(flat, f32), dma((PL + 1,))],
        compiler_params=pltpu.CompilerParams(vmem_limit_bytes=32 * 2**20),
    )(*parts)
    return out.reshape(state_field.shape), rhs.reshape(state_field.shape)


def solution(mesh):
    spec = P(None, "gx", "gy")
    return jax.shard_map(shards, mesh=mesh, in_specs=(spec,) * 4, out_specs=(spec, spec), check_vma=False)
```

```python
import jax
import jax.numpy as jnp
from jax import lax
from jax.experimental import pallas as pl
from jax.experimental.pallas import tpu as pltpu
from jax.sharding import PartitionSpec as P

MESH = pl.DeviceIdType.MESH
PL = 4
R = 32
W = 512
NB = 32
NQ = 4
SOLVERS = (0, 5, 2, 7)
NS = 4
PG = 16 // NS
NA = 6
NV = 4


def sweep_kernel(u_hbm, kx_hbm, ky_hbm, g_hbm, r_ref, a_s, b_s, v_s, xf,
                 u_ref, kx_ref, ky_ref, g_ref,
                 cols_s, hcol, es,
                 ik_s, r_s, msg, inbox, msg2, inbox2, dmat, gmat, res,
                 ls, hs, hr, ms, mr, rs, rr):
    loads = [pltpu.make_async_copy(src, dst, ls.at[i]) for i, (src, dst) in enumerate(
        ((u_hbm, u_ref), (ky_hbm, ky_ref), (kx_hbm, kx_ref), (g_hbm, g_ref)))]
    for load in loads:
        load.start()
    me = lax.axis_index("gx")
    gy = lax.axis_index("gy")
    west, east = lax.rem(gy + 7, 8), lax.rem(gy + 1, 8)

    def signal(dev):
        pl.semaphore_signal(barrier, inc=1, device_id=dev, device_id_type=MESH)

    barrier = pltpu.get_barrier_semaphore()
    slot = jnp.int32(NS)
    for s in range(NS):
        slot = jnp.where(me == SOLVERS[s], s, slot)
    is_solver = slot < NS

    @pl.when(is_solver)
    def _():
        for k in range(1, NB):
            signal((lax.rem(me + k, NB), gy))

    for dev in ((me, west), (me, east)):
        signal(dev)

    loads[0].wait()
    loads[1].wait()

    lane = lax.broadcasted_iota(jnp.int32, (8, 128), 1)
    kyf = ky_ref[...].astype(jnp.float32)
    to_east = jnp.zeros((8, 128), jnp.float32)
    to_west = jnp.zeros((8, 128), jnp.float32)
    for m in range(16):
        sl = slice(8 * m, 8 * m + 8)
        to_east = jnp.where(lane == m, pltpu.roll(u_ref[sl, 384:512], (m + 1) % 128, 1), to_east)
        to_east = jnp.where(lane == 16 + m, pltpu.roll(kyf[sl, 384:512], (m + 17) % 128, 1), to_east)
        to_west = jnp.where(lane == m, pltpu.roll(u_ref[sl, 0:128], m, 1) if m else u_ref[sl, 0:128], to_west)
    cols_s[0] = to_east
    cols_s[1] = to_west

    pl.semaphore_wait(barrier, 2 + NS - is_solver.astype(jnp.int32))

    def send(src, dst, i, dev):
        c = pltpu.make_async_remote_copy(src_ref=src, dst_ref=dst, send_sem=hs.at[i], recv_sem=hr.at[i],
                                         device_id=dev, device_id_type=MESH)
        c.start()
        return c

    halos = [send(cols_s.at[0], hcol.at[0], 0, (me, east)), send(cols_s.at[1], hcol.at[1], 1, (me, west))]

    loads[2].wait()
    ik = 1.0 / kx_ref[...].astype(jnp.float32)
    for q in range(NQ):
        ik_s[128 * q:128 * q + 128, :] = ik[:, 128 * q:128 * q + 128]
    a = d = jnp.ones((16, 128), jnp.float32)
    b = c = jnp.zeros((16, 128), jnp.float32)
    for i in range(R):
        row = pl.ds(i, 16, stride=R)
        a_s[row, :] = a
        b_s[row, :] = b
        ik = ik_s[row, :]
        c = c + a
        a = a + c * ik
        d = d + b
        b = b + d * ik

    boxes = ((msg, inbox), (msg2, inbox2))

    def put(half, k, value):
        for s in range(NS):
            boxes[half][0][s, PG * k:PG * k + PG, :] = value[PG * s:PG * s + PG, :]

    def map_copy(half, s):
        source, target = boxes[half]
        return pltpu.make_async_remote_copy(
            src_ref=source.at[s], dst_ref=target.at[me],
            send_sem=ms.at[half, s], recv_sem=mr.at[half], device_id=(SOLVERS[s], gy), device_id_type=MESH)

    def send_maps(half):
        for s in range(NS):
            @pl.when(slot != s)
            def _():
                map_copy(half, s).start()

            @pl.when(slot == s)
            def _():
                boxes[half][1][SOLVERS[s]] = boxes[half][0][s]

    for k, value in enumerate((a, b, c)):
        put(0, k, value)
    loads[3].wait()
    for p in range(PL):
        for k, row in ((0, R * p), (1, R * p + R - 1)):
            line = 0.25 * g_ref[row // 16 * 16:row // 16 * 16 + 16, :].astype(jnp.float32)[row % 16:row % 16 + 1, :]
            for q in range(NQ):
                es[k, PL * q + p:PL * q + p + 1, :] = line[:, 128 * q:128 * q + 128]
    put(0, 3, es[0])
    put(0, 4, es[1])
    put(0, 5, ik_s[pl.ds(R - 1, 16, stride=R), :])
    send_maps(0)

    for h in halos:
        h.wait()

    lane_w = lax.broadcasted_iota(jnp.int32, (R, W), 1)
    row_w = lax.broadcasted_iota(jnp.int32, (R, W), 0)
    col_w = jnp.where(gy == 0, 0.0, hcol[0])
    col_e = jnp.where(gy == 7, 0.0, hcol[1])

    def wide(tile, at_end):
        rest = jnp.zeros((tile.shape[0], W - 128), jnp.float32)
        return jnp.concatenate([rest, tile] if at_end else [tile, rest], axis=1)

    for p in range(PL):
        sl = slice(R * p, R * p + R)
        u = u_ref[sl, :]
        ky = ky_ref[sl, :].astype(jnp.float32)
        g = g_ref[sl, :].astype(jnp.float32)
        cw, ck, ce = [], [], []
        for q in range(4):
            m = 4 * p + q
            cw.append(pltpu.roll(col_w, 128 - m, 1) if m else col_w)
            ck.append(pltpu.roll(col_w, 112 - m, 1))
            ce.append(pltpu.roll(col_e, 127 - m, 1))
        cw, ck, ce = (jnp.concatenate(t, axis=0) for t in (cw, ck, ce))
        uw = jnp.where(lane_w == 0, wide(cw, False), pltpu.roll(u, 1, 1))
        kb = jnp.where(lane_w == 0, wide(ck, False), pltpu.roll(ky, 1, 1))
        ue = jnp.where(lane_w == W - 1, wide(ce, True), pltpu.roll(u, W - 1, 1))
        dd = ue - uw
        for k, row in ((2, 0), (3, R - 1)):
            for q in range(NQ):
                es[k, PL * q + p:PL * q + p + 1, :] = dd[row:row + 1, 128 * q:128 * q + 128]
        up = jnp.where(row_w == 0, 0.0, pltpu.roll(dd, 1, 0))
        dn = jnp.where(row_w == R - 1, 0.0, pltpu.roll(dd, R - 1, 0))
        right = u + (ky * (ue - u) - kb * (u - uw)) + g * (dn - up) * 0.25
        r_ref[sl, :] = right
        for q in range(NQ):
            r_s[128 * q + R * p:128 * q + R * p + R, :] = right[:, 128 * q:128 * q + 128]

    vx = vf = jnp.zeros((16, 128), jnp.float32)
    for i in range(R):
        row = pl.ds(i, 16, stride=R)
        v_s[row, :] = vx
        vf = vf + (vx - r_s[row, :])
        vx = vx + vf * ik_s[row, :]
    put(1, 0, vx)
    put(1, 1, vf)

    put(1, 2, es[2])
    put(1, 3, es[3])
    send_maps(1)

    @pl.when(is_solver)
    def _():
        def arrived(half):
            part = boxes[half][1].at[pl.ds(0, NB - 1)]
            pltpu.make_async_copy(part, part, mr.at[half]).wait()

        def value(half, p, k):
            return boxes[half][1][p, PG * k:PG * k + PG, :]

        def matrix(p):
            a, b, c = (value(0, p, k) for k in range(3))
            return a, b, c, (1.0 + b * c) / a

        def offset(p):
            return [value(1, p, k) for k in range(2)]

        arrived(0)
        groups = []
        for z in range(8):
            a, b, c, d = matrix(4 * z)
            dmat[4 * z] = d
            for x in range(1, 4):
                a2, b2, c2, d2 = matrix(4 * z + x)
                dmat[4 * z + x] = d2
                a, c = a2 * a + b2 * c, c2 * a + d2 * c
                b, d = a2 * b + b2 * d, c2 * b + d2 * d
            groups.append((a, b, c, d))
        zero = jnp.zeros((PG, 128), jnp.float32)
        gl, gr = zero, zero
        gls, grs, invl, invr = [zero], [], [], []
        for z in range(7):
            a, b, c, d = groups[z]
            invl.append(1.0 / (a + b * gl))
            gl = (c + d * gl) * invl[-1]
            gls.append(gl)
        a, b, c, d = groups[7]
        invr.append(1.0 / b)
        gr = a * invr[0]
        grs.append(gr)
        for z in range(6, -1, -1):
            a, b, c, d = groups[z]
            invr.insert(0, 1.0 / (d + gr * b))
            gr = (c + gr * a) * invr[0]
            grs.insert(0, gr)
        for z in range(8):
            gmat[0, z] = gls[z]
            gmat[1, z] = grs[z]
            gmat[2, z] = invl[z] if z < 7 else zero
            gmat[3, z] = invr[z]
            gmat[4, z] = 1.0 / (gls[z] + grs[z])

        arrived(1)
        for p in range(NB):
            first = -value(0, p, 3) * value(1, p - 1, 3) if p > 0 else zero
            last = value(0, p, 4) * value(1, p + 1, 2) if p < NB - 1 else zero
            vx, vf = offset(p)
            inbox2[p, 0:PG, :] = vx - (value(0, p, 1) * first + value(0, p, 5) * last)
            inbox2[p, PG:2 * PG, :] = vf - (dmat[p] * first + last)
            res[p, 2 * PG:3 * PG, :] = first
            res[p, 3 * PG:4 * PG, :] = last

        def block(p):
            a, b, c = (value(0, p, k) for k in range(3))
            return a, b, c, dmat[p], *offset(p)

        sums = []
        for z in range(8):
            vx, vf = offset(4 * z)
            for x in range(1, 4):
                a2, b2, c2, d2, vx2, vf2 = block(4 * z + x)
                vx, vf = a2 * vx + b2 * vf + vx2, c2 * vx + d2 * vf + vf2
            sums.append((vx, vf))
        left, right = [zero], []
        for z in range(7):
            vx, vf = sums[z]
            left.append(left[-1] * gmat[2, z] + vf - gmat[0, z + 1] * vx)
        right.append(-sums[7][0] * gmat[3, 7])
        for z in range(6, -1, -1):
            vx, vf = sums[z]
            right.insert(0, (right[0] - vf - gmat[1, z + 1] * vx) * gmat[3, z])
        for z in range(8):
            x0 = (right[z] - left[z]) * gmat[4, z]
            f0 = gmat[0, z] * x0 + left[z]
            for x in range(4):
                p = 4 * z + x
                res[p, 0:PG, :] = x0
                res[p, PG:2 * PG, :] = f0
                if x < 3:
                    a, b, c, d, vx, vf = block(p)
                    x0, f0 = a * x0 + b * f0 + vx, c * x0 + d * f0 + vf

        for p in range(NB):
            @pl.when(me != p)
            def _():
                pltpu.make_async_remote_copy(
                    src_ref=res.at[p], dst_ref=xf.at[slot],
                    send_sem=rs, recv_sem=rr.at[slot], device_id=(p, gy), device_id_type=MESH).start()
        for s in range(NS):
            @pl.when(slot == s)
            def _():
                xf[s] = res[SOLVERS[s]]

    for s in range(NS):
        @pl.when(slot != s)
        def _():
            pltpu.make_async_copy(xf.at[s], xf.at[s], rr.at[s]).wait()

    for p in range(PL):
        for k, row in ((2, R * p), (3, R * p + R - 1)):
            for q in range(NQ):
                s, h = divmod(PL * q + p, PG)
                at = (slice(row, row + 1), slice(128 * q, 128 * q + 128))
                r_ref[at] = r_ref[at] + xf[s, PG * k + h:PG * k + h + 1, :]

    for s in range(NS):
        @pl.when(slot != s)
        def _():
            map_copy(0, s).wait_send()
            map_copy(1, s).wait_send()

    @pl.when(is_solver)
    def _():
        part = res.at[pl.ds(0, NB - 1)]
        pltpu.make_async_copy(part, part, rs).wait()


def finish_kernel(r_ref, a_ref, b_ref, v_ref, xf_ref, o_hbm, r_hbm, o_ref, sems):
    right = pltpu.make_async_copy(r_ref, r_hbm, sems.at[PL])
    right.start()
    copies = []
    for p in range(PL):
        sl = slice(R * p, R * p + R)
        for q in range(NQ):
            s, h = divmod(PL * q + p, PG)
            x0 = xf_ref[s, h:h + 1, :]
            f0 = xf_ref[s, PG + h:PG + h + 1, :] - xf_ref[s, 2 * PG + h:2 * PG + h + 1, :]
            ts = slice(128 * q + R * p, 128 * q + R * p + R)
            o_ref[sl, 128 * q:128 * q + 128] = a_ref[ts, :] * x0 + b_ref[ts, :] * f0 + v_ref[ts, :]
        part = pl.ds(R * p, R)
        copies.append(pltpu.make_async_copy(o_ref.at[part], o_hbm.at[part], sems.at[p]))
        copies[-1].start()
    for copy in copies:
        copy.wait()
    right.wait()


def shards(state_field, x_coupling, y_coupling, cross_coeff):
    flat = (PL * R, W)
    vmem = pl.BlockSpec(memory_space=pltpu.VMEM)
    hbm = pl.BlockSpec(memory_space=pltpu.HBM)
    f32, bf16 = jnp.float32, jnp.bfloat16
    tiles = (NQ * PL * R, 128)
    big = pltpu.VMEM(tiles, f32)
    dma = pltpu.SemaphoreType.DMA
    shape = jax.ShapeDtypeStruct
    args = [pltpu.with_memory_space_constraint(x.reshape(flat), pltpu.HBM)
            for x in (state_field, x_coupling, y_coupling, cross_coeff)]
    parts = pl.pallas_call(
        sweep_kernel,
        out_shape=(shape(flat, f32), shape(tiles, f32), shape(tiles, f32), shape(tiles, f32),
                   shape((NS, 4 * PG, 128), f32)),
        in_specs=[hbm] * 4,
        out_specs=(vmem,) * 5,
        scratch_shapes=[
            pltpu.VMEM(flat, f32), pltpu.VMEM(flat, bf16), pltpu.VMEM(flat, bf16), pltpu.VMEM(flat, bf16),
            pltpu.VMEM((2, 8, 128), f32), pltpu.VMEM((2, 8, 128), f32), pltpu.VMEM((4, 16, 128), f32),
            big, big,
            pltpu.VMEM((NS, PG * NA, 128), f32), pltpu.VMEM((NB, PG * NA, 128), f32),
            pltpu.VMEM((NS, PG * NV, 128), f32), pltpu.VMEM((NB, PG * NV, 128), f32),
            pltpu.VMEM((NB, PG, 128), f32), pltpu.VMEM((5, 8, PG, 128), f32),
            pltpu.VMEM((NB, 4 * PG, 128), f32),
            dma((4,)), dma((2,)), dma((2,)), dma((2, NS)), dma((2,)), dma(()), dma((NS,)),
        ],
        compiler_params=pltpu.CompilerParams(
            collective_id=0, has_side_effects=True, vmem_limit_bytes=32 * 2**20),
    )(*args)
    out, rhs = pl.pallas_call(
        finish_kernel,
        out_shape=(shape(flat, f32),) * 2,
        in_specs=[vmem] * 5,
        out_specs=(hbm, hbm),
        scratch_shapes=[pltpu.VMEM(flat, f32), dma((PL + 1,))],
        compiler_params=pltpu.CompilerParams(vmem_limit_bytes=32 * 2**20),
    )(*parts)
    return out.reshape(state_field.shape), rhs.reshape(state_field.shape)


def solution(mesh):
    spec = P(None, "gx", "gy")
    return jax.shard_map(shards, mesh=mesh, in_specs=(spec,) * 4, out_specs=(spec, spec), check_vma=False)
```

```python
import jax
import jax.numpy as jnp
from jax import lax
from jax.experimental import pallas as pl
from jax.experimental.pallas import tpu as pltpu
from jax.sharding import PartitionSpec as P

MESH = pl.DeviceIdType.MESH
PL = 4
R = 32
W = 512
NB = 32
NQ = 4
NS = 4
PG = 16 // NS
NA = 6
NV = 4


def sweep_kernel(u_hbm, kx_hbm, ky_hbm, g_hbm, r_ref, a_s, b_s, v_s, xf,
                 u_ref, kx_ref, ky_ref, g_ref,
                 cols_s, hcol, es,
                 ik_s, r_s, msg, inbox, msg2, inbox2, dmat, gmat, res,
                 ls, hs, hr, ms, mr, rs, rr):
    loads = [pltpu.make_async_copy(src, dst, ls.at[i]) for i, (src, dst) in enumerate(
        ((u_hbm, u_ref), (ky_hbm, ky_ref), (kx_hbm, kx_ref), (g_hbm, g_ref)))]
    for load in loads:
        load.start()
    me = lax.axis_index("gx")
    gy = lax.axis_index("gy")
    west, east = lax.rem(gy + 7, 8), lax.rem(gy + 1, 8)

    def signal(dev):
        pl.semaphore_signal(barrier, inc=1, device_id=dev, device_id_type=MESH)

    barrier = pltpu.get_barrier_semaphore()
    base = NS * lax.rem(gy, 2)
    slot = jnp.where((me >= base) & (me < base + NS), me - base, NS)
    is_solver = slot < NS

    @pl.when(is_solver)
    def _():
        for k in range(1, NB):
            signal((lax.rem(me + k, NB), gy))

    for dev in ((me, west), (me, east)):
        signal(dev)

    loads[0].wait()
    loads[1].wait()

    lane = lax.broadcasted_iota(jnp.int32, (8, 128), 1)
    kyf = ky_ref[...].astype(jnp.float32)
    to_east = jnp.zeros((8, 128), jnp.float32)
    to_west = jnp.zeros((8, 128), jnp.float32)
    for m in range(16):
        sl = slice(8 * m, 8 * m + 8)
        to_east = jnp.where(lane == m, pltpu.roll(u_ref[sl, 384:512], (m + 1) % 128, 1), to_east)
        to_east = jnp.where(lane == 16 + m, pltpu.roll(kyf[sl, 384:512], (m + 17) % 128, 1), to_east)
        to_west = jnp.where(lane == m, pltpu.roll(u_ref[sl, 0:128], m, 1) if m else u_ref[sl, 0:128], to_west)
    cols_s[0] = to_east
    cols_s[1] = to_west

    loads[2].wait()
    ik = 1.0 / kx_ref[...].astype(jnp.float32)
    for q in range(NQ):
        ik_s[128 * q:128 * q + 128, :] = ik[:, 128 * q:128 * q + 128]
    a = d = jnp.ones((16, 128), jnp.float32)
    b = c = jnp.zeros((16, 128), jnp.float32)
    for i in range(R):
        row = pl.ds(i, 16, stride=R)
        a_s[row, :] = a
        b_s[row, :] = b
        ik = ik_s[row, :]
        c = c + a
        a = a + c * ik
        d = d + b
        b = b + d * ik

    boxes = ((msg, inbox), (msg2, inbox2))

    def put(half, k, value):
        for s in range(NS):
            boxes[half][0][s, PG * k:PG * k + PG, :] = value[PG * s:PG * s + PG, :]

    def map_copy(half, s):
        source, target = boxes[half]
        return pltpu.make_async_remote_copy(
            src_ref=source.at[s], dst_ref=target.at[me],
            send_sem=ms.at[half, s], recv_sem=mr.at[half], device_id=(base + s, gy), device_id_type=MESH)

    def send_maps(half):
        for k in (2, 1, 3, 0):
            far = lax.rem(me + k, NS)

            @pl.when(slot != far)
            def _():
                map_copy(half, far).start()

        for s in range(NS):
            @pl.when(slot == s)
            def _():
                boxes[half][1][me] = boxes[half][0][s]

    for k, value in enumerate((a, b, c)):
        put(0, k, value)
    loads[3].wait()
    for p in range(PL):
        for k, row in ((0, R * p), (1, R * p + R - 1)):
            line = 0.25 * g_ref[row // 16 * 16:row // 16 * 16 + 16, :].astype(jnp.float32)[row % 16:row % 16 + 1, :]
            for q in range(NQ):
                es[k, PL * q + p:PL * q + p + 1, :] = line[:, 128 * q:128 * q + 128]
    put(0, 3, es[0])
    put(0, 4, es[1])
    put(0, 5, ik_s[pl.ds(R - 1, 16, stride=R), :])

    pl.semaphore_wait(barrier, 2 + NS - is_solver.astype(jnp.int32))

    def send(src, dst, i, dev):
        c = pltpu.make_async_remote_copy(src_ref=src, dst_ref=dst, send_sem=hs.at[i], recv_sem=hr.at[i],
                                         device_id=dev, device_id_type=MESH)
        c.start()
        return c

    halos = [send(cols_s.at[0], hcol.at[0], 0, (me, east)), send(cols_s.at[1], hcol.at[1], 1, (me, west))]

    send_maps(0)

    for h in halos:
        h.wait()

    lane_w = lax.broadcasted_iota(jnp.int32, (R, W), 1)
    row_w = lax.broadcasted_iota(jnp.int32, (R, W), 0)
    col_w = jnp.where(gy == 0, 0.0, hcol[0])
    col_e = jnp.where(gy == 7, 0.0, hcol[1])

    def wide(tile, at_end):
        rest = jnp.zeros((tile.shape[0], W - 128), jnp.float32)
        return jnp.concatenate([rest, tile] if at_end else [tile, rest], axis=1)

    for p in range(PL):
        sl = slice(R * p, R * p + R)
        u = u_ref[sl, :]
        ky = ky_ref[sl, :].astype(jnp.float32)
        g = g_ref[sl, :].astype(jnp.float32)
        cw, ck, ce = [], [], []
        for q in range(4):
            m = 4 * p + q
            cw.append(pltpu.roll(col_w, 128 - m, 1) if m else col_w)
            ck.append(pltpu.roll(col_w, 112 - m, 1))
            ce.append(pltpu.roll(col_e, 127 - m, 1))
        cw, ck, ce = (jnp.concatenate(t, axis=0) for t in (cw, ck, ce))
        uw = jnp.where(lane_w == 0, wide(cw, False), pltpu.roll(u, 1, 1))
        kb = jnp.where(lane_w == 0, wide(ck, False), pltpu.roll(ky, 1, 1))
        ue = jnp.where(lane_w == W - 1, wide(ce, True), pltpu.roll(u, W - 1, 1))
        dd = ue - uw
        for k, row in ((2, 0), (3, R - 1)):
            for q in range(NQ):
                es[k, PL * q + p:PL * q + p + 1, :] = dd[row:row + 1, 128 * q:128 * q + 128]
        up = jnp.where(row_w == 0, 0.0, pltpu.roll(dd, 1, 0))
        dn = jnp.where(row_w == R - 1, 0.0, pltpu.roll(dd, R - 1, 0))
        right = u + (ky * (ue - u) - kb * (u - uw)) + g * (dn - up) * 0.25
        r_ref[sl, :] = right
        for q in range(NQ):
            r_s[128 * q + R * p:128 * q + R * p + R, :] = right[:, 128 * q:128 * q + 128]

    vx = vf = jnp.zeros((16, 128), jnp.float32)
    for i in range(R):
        row = pl.ds(i, 16, stride=R)
        v_s[row, :] = vx
        vf = vf + (vx - r_s[row, :])
        vx = vx + vf * ik_s[row, :]
    put(1, 0, vx)
    put(1, 1, vf)

    put(1, 2, es[2])
    put(1, 3, es[3])
    send_maps(1)

    @pl.when(is_solver)
    def _():
        def arrived(half):
            part = boxes[half][1].at[pl.ds(0, NB - 1)]
            pltpu.make_async_copy(part, part, mr.at[half]).wait()

        def value(half, p, k):
            return boxes[half][1][p, PG * k:PG * k + PG, :]

        def matrix(p):
            a, b, c = (value(0, p, k) for k in range(3))
            return a, b, c, (1.0 + b * c) / a

        def offset(p):
            return [value(1, p, k) for k in range(2)]

        arrived(0)
        groups = []
        for z in range(8):
            a, b, c, d = matrix(4 * z)
            dmat[4 * z] = d
            for x in range(1, 4):
                a2, b2, c2, d2 = matrix(4 * z + x)
                dmat[4 * z + x] = d2
                a, c = a2 * a + b2 * c, c2 * a + d2 * c
                b, d = a2 * b + b2 * d, c2 * b + d2 * d
            groups.append((a, b, c, d))
        zero = jnp.zeros((PG, 128), jnp.float32)
        gl, gr = zero, zero
        gls, grs, invl, invr = [zero], [], [], []
        for z in range(7):
            a, b, c, d = groups[z]
            invl.append(1.0 / (a + b * gl))
            gl = (c + d * gl) * invl[-1]
            gls.append(gl)
        a, b, c, d = groups[7]
        invr.append(1.0 / b)
        gr = a * invr[0]
        grs.append(gr)
        for z in range(6, -1, -1):
            a, b, c, d = groups[z]
            invr.insert(0, 1.0 / (d + gr * b))
            gr = (c + gr * a) * invr[0]
            grs.insert(0, gr)
        for z in range(8):
            gmat[0, z] = gls[z]
            gmat[1, z] = grs[z]
            gmat[2, z] = invl[z] if z < 7 else zero
            gmat[3, z] = invr[z]
            gmat[4, z] = 1.0 / (gls[z] + grs[z])

        arrived(1)
        for p in range(NB):
            first = -value(0, p, 3) * value(1, p - 1, 3) if p > 0 else zero
            last = value(0, p, 4) * value(1, p + 1, 2) if p < NB - 1 else zero
            vx, vf = offset(p)
            inbox2[p, 0:PG, :] = vx - (value(0, p, 1) * first + value(0, p, 5) * last)
            inbox2[p, PG:2 * PG, :] = vf - (dmat[p] * first + last)
            res[p, 2 * PG:3 * PG, :] = first
            res[p, 3 * PG:4 * PG, :] = last

        def block(p):
            a, b, c = (value(0, p, k) for k in range(3))
            return a, b, c, dmat[p], *offset(p)

        sums = []
        for z in range(8):
            vx, vf = offset(4 * z)
            for x in range(1, 4):
                a2, b2, c2, d2, vx2, vf2 = block(4 * z + x)
                vx, vf = a2 * vx + b2 * vf + vx2, c2 * vx + d2 * vf + vf2
            sums.append((vx, vf))
        left, right = [zero], []
        for z in range(7):
            vx, vf = sums[z]
            left.append(left[-1] * gmat[2, z] + vf - gmat[0, z + 1] * vx)
        right.append(-sums[7][0] * gmat[3, 7])
        for z in range(6, -1, -1):
            vx, vf = sums[z]
            right.insert(0, (right[0] - vf - gmat[1, z + 1] * vx) * gmat[3, z])
        for z in range(8):
            x0 = (right[z] - left[z]) * gmat[4, z]
            f0 = gmat[0, z] * x0 + left[z]
            for x in range(4):
                p = 4 * z + x
                res[p, 0:PG, :] = x0
                res[p, PG:2 * PG, :] = f0
                if x < 3:
                    a, b, c, d, vx, vf = block(p)
                    x0, f0 = a * x0 + b * f0 + vx, c * x0 + d * f0 + vf

        for p in range(NB):
            @pl.when(me != p)
            def _():
                pltpu.make_async_remote_copy(
                    src_ref=res.at[p], dst_ref=xf.at[slot],
                    send_sem=rs, recv_sem=rr.at[slot], device_id=(p, gy), device_id_type=MESH).start()
        for s in range(NS):
            @pl.when(slot == s)
            def _():
                xf[s] = res[me]

    for s in range(NS):
        @pl.when(slot != s)
        def _():
            pltpu.make_async_copy(xf.at[s], xf.at[s], rr.at[s]).wait()

    for p in range(PL):
        for k, row in ((2, R * p), (3, R * p + R - 1)):
            for q in range(NQ):
                s, h = divmod(PL * q + p, PG)
                at = (slice(row, row + 1), slice(128 * q, 128 * q + 128))
                r_ref[at] = r_ref[at] + xf[s, PG * k + h:PG * k + h + 1, :]

    for s in range(NS):
        @pl.when(slot != s)
        def _():
            map_copy(0, s).wait_send()
            map_copy(1, s).wait_send()

    @pl.when(is_solver)
    def _():
        part = res.at[pl.ds(0, NB - 1)]
        pltpu.make_async_copy(part, part, rs).wait()


def finish_kernel(r_ref, a_ref, b_ref, v_ref, xf_ref, o_hbm, r_hbm, o_ref, sems):
    right = pltpu.make_async_copy(r_ref, r_hbm, sems.at[PL])
    right.start()
    copies = []
    for p in range(PL):
        sl = slice(R * p, R * p + R)
        for q in range(NQ):
            s, h = divmod(PL * q + p, PG)
            x0 = xf_ref[s, h:h + 1, :]
            f0 = xf_ref[s, PG + h:PG + h + 1, :] - xf_ref[s, 2 * PG + h:2 * PG + h + 1, :]
            ts = slice(128 * q + R * p, 128 * q + R * p + R)
            o_ref[sl, 128 * q:128 * q + 128] = a_ref[ts, :] * x0 + b_ref[ts, :] * f0 + v_ref[ts, :]
        part = pl.ds(R * p, R)
        copies.append(pltpu.make_async_copy(o_ref.at[part], o_hbm.at[part], sems.at[p]))
        copies[-1].start()
    for copy in copies:
        copy.wait()
    right.wait()


def shards(state_field, x_coupling, y_coupling, cross_coeff):
    flat = (PL * R, W)
    vmem = pl.BlockSpec(memory_space=pltpu.VMEM)
    hbm = pl.BlockSpec(memory_space=pltpu.HBM)
    f32, bf16 = jnp.float32, jnp.bfloat16
    tiles = (NQ * PL * R, 128)
    big = pltpu.VMEM(tiles, f32)
    dma = pltpu.SemaphoreType.DMA
    shape = jax.ShapeDtypeStruct
    args = [pltpu.with_memory_space_constraint(x.reshape(flat), pltpu.HBM)
            for x in (state_field, x_coupling, y_coupling, cross_coeff)]
    parts = pl.pallas_call(
        sweep_kernel,
        out_shape=(shape(flat, f32), shape(tiles, f32), shape(tiles, f32), shape(tiles, f32),
                   shape((NS, 4 * PG, 128), f32)),
        in_specs=[hbm] * 4,
        out_specs=(vmem,) * 5,
        scratch_shapes=[
            pltpu.VMEM(flat, f32), pltpu.VMEM(flat, bf16), pltpu.VMEM(flat, bf16), pltpu.VMEM(flat, bf16),
            pltpu.VMEM((2, 8, 128), f32), pltpu.VMEM((2, 8, 128), f32), pltpu.VMEM((4, 16, 128), f32),
            big, big,
            pltpu.VMEM((NS, PG * NA, 128), f32), pltpu.VMEM((NB, PG * NA, 128), f32),
            pltpu.VMEM((NS, PG * NV, 128), f32), pltpu.VMEM((NB, PG * NV, 128), f32),
            pltpu.VMEM((NB, PG, 128), f32), pltpu.VMEM((5, 8, PG, 128), f32),
            pltpu.VMEM((NB, 4 * PG, 128), f32),
            dma((4,)), dma((2,)), dma((2,)), dma((2, NS)), dma((2,)), dma(()), dma((NS,)),
        ],
        compiler_params=pltpu.CompilerParams(
            collective_id=0, has_side_effects=True, vmem_limit_bytes=32 * 2**20),
    )(*args)
    out, rhs = pl.pallas_call(
        finish_kernel,
        out_shape=(shape(flat, f32),) * 2,
        in_specs=[vmem] * 5,
        out_specs=(hbm, hbm),
        scratch_shapes=[pltpu.VMEM(flat, f32), dma((PL + 1,))],
        compiler_params=pltpu.CompilerParams(vmem_limit_bytes=32 * 2**20),
    )(*parts)
    return out.reshape(state_field.shape), rhs.reshape(state_field.shape)


def solution(mesh):
    spec = P(None, "gx", "gy")
    return jax.shard_map(shards, mesh=mesh, in_specs=(spec,) * 4, out_specs=(spec, spec), check_vma=False)
```

```python
import jax
import jax.numpy as jnp
from jax import lax
from jax.experimental import pallas as pl
from jax.experimental.pallas import tpu as pltpu
from jax.sharding import PartitionSpec as P

MESH = pl.DeviceIdType.MESH
PL = 4
R = 32
W = 512
NB = 32
NQ = 4
NS = 4
PG = 16 // NS
NA = 6
NV = 4


def sweep_kernel(u_hbm, kx_hbm, ky_hbm, g_hbm, r_ref, a_s, b_s, v_s, xf,
                 u_ref, kx_ref, ky_ref, g_ref,
                 cols_s, hcol, es,
                 ik_s, r_s, msg, inbox, msg2, inbox2, dmat, gmat, res,
                 ls, hs, hr, ms, mr, rs, rr):
    me = lax.axis_index("gx")
    gy = lax.axis_index("gy")
    west, east = lax.rem(gy + 7, 8), lax.rem(gy + 1, 8)

    def signal(dev):
        pl.semaphore_signal(barrier, inc=1, device_id=dev, device_id_type=MESH)

    barrier = pltpu.get_barrier_semaphore()
    base = NS * lax.rem(gy, 2)
    slot = jnp.where((me >= base) & (me < base + NS), me - base, NS)
    is_solver = slot < NS

    for dev in ((me, west), (me, east)):
        signal(dev)

    loads = [pltpu.make_async_copy(src, dst, ls.at[i]) for i, (src, dst) in enumerate(
        ((u_hbm, u_ref), (ky_hbm, ky_ref), (kx_hbm, kx_ref), (g_hbm, g_ref)))]
    for load in loads:
        load.start()

    @pl.when(is_solver)
    def _():
        for k in range(1, NB):
            signal((lax.rem(me + k, NB), gy))

    loads[0].wait()
    loads[1].wait()

    lane = lax.broadcasted_iota(jnp.int32, (8, 128), 1)
    kyf = ky_ref[...].astype(jnp.float32)
    to_east = jnp.zeros((8, 128), jnp.float32)
    to_west = jnp.zeros((8, 128), jnp.float32)
    for m in range(16):
        sl = slice(8 * m, 8 * m + 8)
        to_east = jnp.where(lane == m, pltpu.roll(u_ref[sl, 384:512], (m + 1) % 128, 1), to_east)
        to_east = jnp.where(lane == 16 + m, pltpu.roll(kyf[sl, 384:512], (m + 17) % 128, 1), to_east)
        to_west = jnp.where(lane == m, pltpu.roll(u_ref[sl, 0:128], m, 1) if m else u_ref[sl, 0:128], to_west)
    cols_s[0] = to_east
    cols_s[1] = to_west

    pl.semaphore_wait(barrier, 2 + NS - is_solver.astype(jnp.int32))

    def send(src, dst, i, dev):
        c = pltpu.make_async_remote_copy(src_ref=src, dst_ref=dst, send_sem=hs.at[i], recv_sem=hr.at[i],
                                         device_id=dev, device_id_type=MESH)
        c.start()
        return c

    halos = [send(cols_s.at[0], hcol.at[0], 0, (me, east)), send(cols_s.at[1], hcol.at[1], 1, (me, west))]

    loads[2].wait()
    ik = 1.0 / kx_ref[...].astype(jnp.float32)
    for q in range(NQ):
        ik_s[128 * q:128 * q + 128, :] = ik[:, 128 * q:128 * q + 128]
    a = d = jnp.ones((16, 128), jnp.float32)
    b = c = jnp.zeros((16, 128), jnp.float32)
    for i in range(R):
        row = pl.ds(i, 16, stride=R)
        a_s[row, :] = a
        b_s[row, :] = b
        ik = ik_s[row, :]
        c = c + a
        a = a + c * ik
        d = d + b
        b = b + d * ik

    boxes = ((msg, inbox), (msg2, inbox2))

    def put(half, k, value):
        for s in range(NS):
            boxes[half][0][s, PG * k:PG * k + PG, :] = value[PG * s:PG * s + PG, :]

    def map_copy(half, s):
        source, target = boxes[half]
        return pltpu.make_async_remote_copy(
            src_ref=source.at[s], dst_ref=target.at[me],
            send_sem=ms.at[half, s], recv_sem=mr.at[half], device_id=(base + s, gy), device_id_type=MESH)

    def send_maps(half):
        for k in (2, 1, 3, 0):
            far = lax.rem(me + k, NS)

            @pl.when(slot != far)
            def _():
                map_copy(half, far).start()

        for s in range(NS):
            @pl.when(slot == s)
            def _():
                boxes[half][1][me] = boxes[half][0][s]

    for k, value in enumerate((a, b, c)):
        put(0, k, value)
    loads[3].wait()
    for p in range(PL):
        for k, row in ((0, R * p), (1, R * p + R - 1)):
            line = 0.25 * g_ref[row // 16 * 16:row // 16 * 16 + 16, :].astype(jnp.float32)[row % 16:row % 16 + 1, :]
            for q in range(NQ):
                es[k, PL * q + p:PL * q + p + 1, :] = line[:, 128 * q:128 * q + 128]
    put(0, 3, es[0])
    put(0, 4, es[1])
    put(0, 5, ik_s[pl.ds(R - 1, 16, stride=R), :])

    send_maps(0)

    for h in halos:
        h.wait()

    lane_w = lax.broadcasted_iota(jnp.int32, (R, W), 1)
    row_w = lax.broadcasted_iota(jnp.int32, (R, W), 0)
    col_w = jnp.where(gy == 0, 0.0, hcol[0])
    col_e = jnp.where(gy == 7, 0.0, hcol[1])

    def wide(tile, at_end):
        rest = jnp.zeros((tile.shape[0], W - 128), jnp.float32)
        return jnp.concatenate([rest, tile] if at_end else [tile, rest], axis=1)

    for p in range(PL):
        sl = slice(R * p, R * p + R)
        u = u_ref[sl, :]
        ky = ky_ref[sl, :].astype(jnp.float32)
        g = g_ref[sl, :].astype(jnp.float32)
        cw, ck, ce = [], [], []
        for q in range(4):
            m = 4 * p + q
            cw.append(pltpu.roll(col_w, 128 - m, 1) if m else col_w)
            ck.append(pltpu.roll(col_w, 112 - m, 1))
            ce.append(pltpu.roll(col_e, 127 - m, 1))
        cw, ck, ce = (jnp.concatenate(t, axis=0) for t in (cw, ck, ce))
        uw = jnp.where(lane_w == 0, wide(cw, False), pltpu.roll(u, 1, 1))
        kb = jnp.where(lane_w == 0, wide(ck, False), pltpu.roll(ky, 1, 1))
        ue = jnp.where(lane_w == W - 1, wide(ce, True), pltpu.roll(u, W - 1, 1))
        dd = ue - uw
        for k, row in ((2, 0), (3, R - 1)):
            for q in range(NQ):
                es[k, PL * q + p:PL * q + p + 1, :] = dd[row:row + 1, 128 * q:128 * q + 128]
        up = jnp.where(row_w == 0, 0.0, pltpu.roll(dd, 1, 0))
        dn = jnp.where(row_w == R - 1, 0.0, pltpu.roll(dd, R - 1, 0))
        right = u + (ky * (ue - u) - kb * (u - uw)) + g * (dn - up) * 0.25
        r_ref[sl, :] = right
        for q in range(NQ):
            r_s[128 * q + R * p:128 * q + R * p + R, :] = right[:, 128 * q:128 * q + 128]

    vx = vf = jnp.zeros((16, 128), jnp.float32)
    for i in range(R):
        row = pl.ds(i, 16, stride=R)
        v_s[row, :] = vx
        vf = vf + (vx - r_s[row, :])
        vx = vx + vf * ik_s[row, :]
    put(1, 0, vx)
    put(1, 1, vf)

    put(1, 2, es[2])
    put(1, 3, es[3])
    send_maps(1)

    @pl.when(is_solver)
    def _():
        def arrived(half):
            part = boxes[half][1].at[pl.ds(0, NB - 1)]
            pltpu.make_async_copy(part, part, mr.at[half]).wait()

        def value(half, p, k):
            return boxes[half][1][p, PG * k:PG * k + PG, :]

        def matrix(p):
            a, b, c = (value(0, p, k) for k in range(3))
            return a, b, c, (1.0 + b * c) / a

        def offset(p):
            return [value(1, p, k) for k in range(2)]

        arrived(0)
        groups = []
        for z in range(8):
            a, b, c, d = matrix(4 * z)
            dmat[4 * z] = d
            for x in range(1, 4):
                a2, b2, c2, d2 = matrix(4 * z + x)
                dmat[4 * z + x] = d2
                a, c = a2 * a + b2 * c, c2 * a + d2 * c
                b, d = a2 * b + b2 * d, c2 * b + d2 * d
            groups.append((a, b, c, d))
        zero = jnp.zeros((PG, 128), jnp.float32)
        gl, gr = zero, zero
        gls, grs, invl, invr = [zero], [], [], []
        for z in range(7):
            a, b, c, d = groups[z]
            invl.append(1.0 / (a + b * gl))
            gl = (c + d * gl) * invl[-1]
            gls.append(gl)
        a, b, c, d = groups[7]
        invr.append(1.0 / b)
        gr = a * invr[0]
        grs.append(gr)
        for z in range(6, -1, -1):
            a, b, c, d = groups[z]
            invr.insert(0, 1.0 / (d + gr * b))
            gr = (c + gr * a) * invr[0]
            grs.insert(0, gr)
        for z in range(8):
            gmat[0, z] = gls[z]
            gmat[1, z] = grs[z]
            gmat[2, z] = invl[z] if z < 7 else zero
            gmat[3, z] = invr[z]
            gmat[4, z] = 1.0 / (gls[z] + grs[z])

        arrived(1)
        for p in range(NB):
            first = -value(0, p, 3) * value(1, p - 1, 3) if p > 0 else zero
            last = value(0, p, 4) * value(1, p + 1, 2) if p < NB - 1 else zero
            vx, vf = offset(p)
            inbox2[p, 0:PG, :] = vx - (value(0, p, 1) * first + value(0, p, 5) * last)
            inbox2[p, PG:2 * PG, :] = vf - (dmat[p] * first + last)
            res[p, 2 * PG:3 * PG, :] = first
            res[p, 3 * PG:4 * PG, :] = last

        def block(p):
            a, b, c = (value(0, p, k) for k in range(3))
            return a, b, c, dmat[p], *offset(p)

        sums = []
        for z in range(8):
            vx, vf = offset(4 * z)
            for x in range(1, 4):
                a2, b2, c2, d2, vx2, vf2 = block(4 * z + x)
                vx, vf = a2 * vx + b2 * vf + vx2, c2 * vx + d2 * vf + vf2
            sums.append((vx, vf))
        left, right = [zero], []
        for z in range(7):
            vx, vf = sums[z]
            left.append(left[-1] * gmat[2, z] + vf - gmat[0, z + 1] * vx)
        right.append(-sums[7][0] * gmat[3, 7])
        for z in range(6, -1, -1):
            vx, vf = sums[z]
            right.insert(0, (right[0] - vf - gmat[1, z + 1] * vx) * gmat[3, z])
        for z in range(8):
            x0 = (right[z] - left[z]) * gmat[4, z]
            f0 = gmat[0, z] * x0 + left[z]
            for x in range(4):
                p = 4 * z + x
                res[p, 0:PG, :] = x0
                res[p, PG:2 * PG, :] = f0
                if x < 3:
                    a, b, c, d, vx, vf = block(p)
                    x0, f0 = a * x0 + b * f0 + vx, c * x0 + d * f0 + vf

        for p in range(NB):
            @pl.when(me != p)
            def _():
                pltpu.make_async_remote_copy(
                    src_ref=res.at[p], dst_ref=xf.at[slot],
                    send_sem=rs, recv_sem=rr.at[slot], device_id=(p, gy), device_id_type=MESH).start()
        for s in range(NS):
            @pl.when(slot == s)
            def _():
                xf[s] = res[me]

    for s in range(NS):
        @pl.when(slot != s)
        def _():
            pltpu.make_async_copy(xf.at[s], xf.at[s], rr.at[s]).wait()

    for p in range(PL):
        for k, row in ((2, R * p), (3, R * p + R - 1)):
            for q in range(NQ):
                s, h = divmod(PL * q + p, PG)
                at = (slice(row, row + 1), slice(128 * q, 128 * q + 128))
                r_ref[at] = r_ref[at] + xf[s, PG * k + h:PG * k + h + 1, :]

    for s in range(NS):
        @pl.when(slot != s)
        def _():
            map_copy(0, s).wait_send()
            map_copy(1, s).wait_send()

    @pl.when(is_solver)
    def _():
        part = res.at[pl.ds(0, NB - 1)]
        pltpu.make_async_copy(part, part, rs).wait()


def finish_kernel(r_ref, a_ref, b_ref, v_ref, xf_ref, o_hbm, r_hbm, o_ref, sems):
    right = pltpu.make_async_copy(r_ref, r_hbm, sems.at[PL])
    right.start()
    copies = []
    for p in range(PL):
        sl = slice(R * p, R * p + R)
        for q in range(NQ):
            s, h = divmod(PL * q + p, PG)
            x0 = xf_ref[s, h:h + 1, :]
            f0 = xf_ref[s, PG + h:PG + h + 1, :] - xf_ref[s, 2 * PG + h:2 * PG + h + 1, :]
            ts = slice(128 * q + R * p, 128 * q + R * p + R)
            o_ref[sl, 128 * q:128 * q + 128] = a_ref[ts, :] * x0 + b_ref[ts, :] * f0 + v_ref[ts, :]
        part = pl.ds(R * p, R)
        copies.append(pltpu.make_async_copy(o_ref.at[part], o_hbm.at[part], sems.at[p]))
        copies[-1].start()
    for copy in copies:
        copy.wait()
    right.wait()


def shards(state_field, x_coupling, y_coupling, cross_coeff):
    flat = (PL * R, W)
    vmem = pl.BlockSpec(memory_space=pltpu.VMEM)
    hbm = pl.BlockSpec(memory_space=pltpu.HBM)
    f32, bf16 = jnp.float32, jnp.bfloat16
    tiles = (NQ * PL * R, 128)
    big = pltpu.VMEM(tiles, f32)
    dma = pltpu.SemaphoreType.DMA
    shape = jax.ShapeDtypeStruct
    args = [pltpu.with_memory_space_constraint(x.reshape(flat), pltpu.HBM)
            for x in (state_field, x_coupling, y_coupling, cross_coeff)]
    parts = pl.pallas_call(
        sweep_kernel,
        out_shape=(shape(flat, f32), shape(tiles, f32), shape(tiles, f32), shape(tiles, f32),
                   shape((NS, 4 * PG, 128), f32)),
        in_specs=[hbm] * 4,
        out_specs=(vmem,) * 5,
        scratch_shapes=[
            pltpu.VMEM(flat, f32), pltpu.VMEM(flat, bf16), pltpu.VMEM(flat, bf16), pltpu.VMEM(flat, bf16),
            pltpu.VMEM((2, 8, 128), f32), pltpu.VMEM((2, 8, 128), f32), pltpu.VMEM((4, 16, 128), f32),
            big, big,
            pltpu.VMEM((NS, PG * NA, 128), f32), pltpu.VMEM((NB, PG * NA, 128), f32),
            pltpu.VMEM((NS, PG * NV, 128), f32), pltpu.VMEM((NB, PG * NV, 128), f32),
            pltpu.VMEM((NB, PG, 128), f32), pltpu.VMEM((5, 8, PG, 128), f32),
            pltpu.VMEM((NB, 4 * PG, 128), f32),
            dma((4,)), dma((2,)), dma((2,)), dma((2, NS)), dma((2,)), dma(()), dma((NS,)),
        ],
        compiler_params=pltpu.CompilerParams(
            collective_id=0, has_side_effects=True, vmem_limit_bytes=32 * 2**20),
    )(*args)
    out, rhs = pl.pallas_call(
        finish_kernel,
        out_shape=(shape(flat, f32),) * 2,
        in_specs=[vmem] * 5,
        out_specs=(hbm, hbm),
        scratch_shapes=[pltpu.VMEM(flat, f32), dma((PL + 1,))],
        compiler_params=pltpu.CompilerParams(vmem_limit_bytes=32 * 2**20),
    )(*parts)
    return out.reshape(state_field.shape), rhs.reshape(state_field.shape)


def solution(mesh):
    spec = P(None, "gx", "gy")
    return jax.shard_map(shards, mesh=mesh, in_specs=(spec,) * 4, out_specs=(spec, spec), check_vma=False)
```
